32 devices in a mesh: gx: 8 (over z, y), gy: 4 (over x, core).
Axes of the slice: x: 2, y: 2, z: 4, core: 2. Of those that a mesh axis runs over, the one named last changes fastest.
Arguments:
- adjoint_trace: bfloat16 [128, 64, 16, 128], P('gx', 'gy'), may hold values from -6 to 6
- coupling: bfloat16 [7, 128, 128], replicated, may hold values from -0.1875 to 0.1875
- log_friction: float32 [64, 64, 128], P('gx', 'gy'), may hold values from -1 to 1
- send_column: int32 [8, 4, 256], P('gx', 'gy'), may hold values from 0 to 255, each once within a row
- live_count: int32 [8, 4, 4], P('gx', 'gy'), may hold values from 0 to 64, as said below
- target_node: int32 [8, 4, 4, 64], P('gx', 'gy'), may hold values from 0 to 127
Outputs:
- trace_update: bfloat16 [128, 64, 16, 128], P('gx', 'gy')
- friction_gradient: float32 [64, 64, 128], P('gx', 'gy')
The draws below stay inside these ranges and needn't reach their ends.
Inputs may be any that keep to these rules, and one draw needn't show every extreme that they name: Each row of send_column lists every local basal face once. `live_count`: in every row of devices along gy, one owner receives 64 live blocks from every device.
All inputs are finite; a program needn't handle non-finite values.
Results may differ from the reference program's by a relative error of at most 0.0059.
Values may be sent and summed in bfloat16 or wider, within the bound.
A program may use at most 64 MiB of HBM per device.

```python
import jax
import jax.numpy as jnp
from jax import lax

TRACE = 128
CX = 16
CY = 16
LAYERS = 16
PX = 8
PY = 16
NB = 256
CAP = 64
NX = 128
NY = 64
MX = 64
MY = 64
N_GX = 8
N_GY = 4


def draw_live_count(key, part):
    first, second, third = jax.random.split(key, 3)
    base = jax.random.randint(first, (N_GX, N_GY, N_GY), 0, CAP + 1)
    level = jax.random.randint(second, (N_GX, N_GY, 1), 1, 5)
    counted = jnp.minimum(base * level // 2, CAP)
    full_owner = jax.random.randint(third, (N_GX, 1, 1), 0, N_GY)
    owners = jnp.arange(N_GY)[None, None, :]
    return jnp.where(owners == full_owner, CAP, counted).astype(jnp.int32)


def set_ends(array, own_key, low, top_value):
    extent = array.shape
    spot = [jax.random.randint(jax.random.fold_in(own_key, axis), (), 0, extent[axis]) for axis in range(len(extent))]
    array = array.at[tuple(spot)].set(low)
    longest = extent.index(max(extent))
    spot[longest] = (spot[longest] + 1) % extent[longest]
    return array.at[tuple(spot)].set(top_value)


def level_of(key, extent, shards, smallest, largest):
    def one(dim, shards_of):
        heights = jax.random.uniform(jax.random.fold_in(jax.random.fold_in(key, 6), dim), (shards_of,), jnp.float32, smallest / len(shards), largest / len(shards))
        return jnp.repeat(jnp.exp(heights), extent[dim] // shards_of).reshape((-1,) + (1,) * (len(extent) - dim - 1))

    factor_of = one(*shards[0])
    for cut in shards[1:]:
        factor_of = factor_of * one(*cut)
    return factor_of


def scatter_about(rng, shape, deviation, most, shards=(), held_as=jnp.bfloat16):
    entries = jax.random.normal(rng, shape, jnp.float32) * deviation
    if len(shards) > 0:
        entries = level_of(rng, shape, shards, -0.22, 0.18) * entries
    return jnp.clip(entries, min=-most, max=most).astype(held_as)


def setup_inputs(seed: int = 0) -> dict:
    key_list = jax.random.split(jax.random.key(seed), 7)
    adjoint_trace = scatter_about(key_list[0], (NX, NY, LAYERS, TRACE), 1.0, 6.0, ((0, 8), (1, 4)))
    coupling = scatter_about(key_list[1], (7, TRACE, TRACE), (7 * TRACE) ** -0.5, 0.1875)
    log_friction = jnp.clip(jax.random.uniform(key_list[2], (MX, MY, TRACE), jnp.float32, -1.0, 1.0) * level_of(key_list[2], (MX, MY, TRACE), ((0, 8), (1, 4)), -0.4, 0.0), -1.0, 1.0)
    send_column = jax.vmap(lambda own: jax.random.permutation(own, NB))(jax.random.split(key_list[3], N_GX * N_GY)).reshape((N_GX, N_GY, NB)).astype(jnp.int32)
    live_count = draw_live_count(jax.random.fold_in(key_list[6], 71), 0)
    target_node = set_ends(jax.random.randint(key_list[5], (N_GX, N_GY, N_GY, CAP), 0, PX * PY), jax.random.fold_in(key_list[5], 1), 0, (PX * PY) - 1).astype(jnp.int32)
    return {"adjoint_trace": adjoint_trace, "coupling": coupling, "log_friction": log_friction, "send_column": send_column, "live_count": live_count, "target_node": target_node}


def couple(extended, coupling):
    own = extended[1:-1, 1:-1]
    rows_a, rows_b, layers_n, width = own.shape
    zeros_layer = jnp.zeros((rows_a, rows_b, 1, width), jnp.bfloat16)
    below = jnp.concatenate([zeros_layer, own[:, :, :-1]], axis=2)
    above = jnp.concatenate([own[:, :, 1:], zeros_layer], axis=2)
    terms = [own, below, above, extended[:-2, 1:-1], extended[2:, 1:-1], extended[1:-1, :-2], extended[1:-1, 2:]]
    total = jnp.zeros((rows_a * rows_b * layers_n, width), jnp.float32)
    for index in range(7):
        total = total + jnp.dot(terms[index].reshape(-1, width), coupling[index], preferred_element_type=jnp.float32)
    return total.reshape(rows_a, rows_b, layers_n, width).astype(jnp.bfloat16)


def stencil(extended):
    center = extended[1:-1, 1:-1]
    beside_all = extended[2:, 1:-1] + extended[:-2, 1:-1] + extended[1:-1, 2:] + extended[1:-1, :-2]
    return 1.3 * center - 0.2 * beside_all


def reference(adjoint_trace, coupling, log_friction, send_column, live_count, target_node):
    padded = jnp.pad(adjoint_trace, ((1, 1), (1, 1), (0, 0), (0, 0)))

    def slab(index):
        extended = lax.dynamic_slice_in_dim(padded, index * CX, CX + 2, 0)
        return couple(extended, coupling)

    trace_update = lax.map(slab, jnp.arange(N_GX).astype(jnp.int32)).reshape(NX, NY, LAYERS, TRACE)
    bottom = trace_update[:, :, 0, :]
    local_faces = bottom.reshape(N_GX, CX, N_GY, CY, TRACE).transpose(0, 2, 1, 3, 4).reshape(N_GX, N_GY, NB, TRACE)
    picked = jnp.take_along_axis(local_faces, send_column[:, :, :, None], axis=2)
    picked = picked.reshape(N_GX, N_GY, N_GY, CAP, TRACE)
    live = jnp.arange(CAP).astype(jnp.int32)[None, None, None, :] < live_count[:, :, :, None]
    tile_nodes = PX * PY
    row_ids = (jnp.arange(N_GX).astype(jnp.int32)[:, None, None, None] * (N_GY * tile_nodes)
               + jnp.arange(N_GY).astype(jnp.int32)[None, None, :, None] * tile_nodes + target_node)
    dump_row = N_GX * N_GY * tile_nodes
    ids = jnp.where(live, row_ids, dump_row).reshape(-1).astype(jnp.int32)
    misfit = jax.ops.segment_sum(picked.reshape(-1, TRACE).astype(jnp.float32), ids, num_segments=dump_row + 1)[:dump_row]
    misfit = misfit.reshape(N_GX, N_GY, PX, PY, TRACE).transpose(0, 2, 1, 3, 4).reshape(MX, MY, TRACE)
    once = stencil(jnp.pad(log_friction, ((1, 1), (1, 1), (0, 0))))
    prior = stencil(jnp.pad(once, ((1, 1), (1, 1), (0, 0))))
    friction_gradient = jnp.exp(log_friction) * misfit + prior
    return trace_update, friction_gradient
```

```python
import functools

import jax
import jax.numpy as jnp
from jax import lax
from jax.experimental import pallas as pl
from jax.experimental.pallas import tpu as pltpu
from jax.sharding import PartitionSpec as P

MESH = pl.DeviceIdType.MESH
BF, F32 = jnp.bfloat16, jnp.float32


def kernel(
    nx, ny, early,
    x_hbm, c_hbm, lf_hbm, sc_hbm, live_hbm, tn_hbm,
    out_ref, grad_ref,
    px, cw, lf, sc, live, tn,
    stage, x0, edge, halo0,
    lf_edge, lf_halo, lf_corner, field, once,
    nodes_out, nodes_in, pick, picked, received,
    local_sem, h0_send, h0_recv, hx_send, hx_recv, lf_send, lf_recv, lc_send, lc_recv,
    nd_send, nd_recv, pk_send, pk_recv,
):
    i, j = lax.axis_index("gx"), lax.axis_index("gy")
    rows, cols, layers, width = x_hbm.shape
    faces = rows * cols
    slots = faces // ny
    tile_a, tile_b = once.shape[0] - 2, cols
    tile_nodes = tile_a * tile_b
    low_a, high_a, low_b, high_b = i > 0, i < nx - 1, j > 0, j < ny - 1
    one = lambda flag: flag.astype(jnp.int32)
    up = lambda v, n: lax.rem(v + 1, n)
    down = lambda v, n: lax.rem(v + n - 1, n)
    to = [(down(i, nx), j), (up(i, nx), j), (i, down(j, ny)), (i, up(j, ny))]
    has_to = [low_a, high_a, low_b, high_b]
    has_from = [high_a, low_a, high_b, low_b]
    corner_to = [(to[a][0], to[2 + b][1]) for a in (0, 1) for b in (0, 1)]
    corner_has_to = [has_to[a] & has_to[2 + b] for a in (0, 1) for b in (0, 1)]
    corner_has_from = [has_from[a] & has_from[2 + b] for a in (0, 1) for b in (0, 1)]

    loads = [
        pltpu.make_async_copy(src, dst, local_sem.at[n])
        for n, (src, dst) in enumerate(
            [
                (x_hbm, px.at[pl.ds(1, rows), pl.ds(1, cols)]),
                (lf_hbm, lf),
                (tn_hbm, tn),
                (live_hbm, live),
                (sc_hbm, sc),
                (c_hbm, cw),
            ]
        )
    ]
    for load in loads:
        load.start()

    barrier = pltpu.get_barrier_semaphore()
    for k in range(1, ny):
        pl.semaphore_signal(barrier, inc=1, device_id=(i, lax.rem(j + k, ny)), device_id_type=MESH)
    for flag, device in list(zip(has_to[:2], to[:2])) + list(zip(corner_has_to, corner_to)):

        @pl.when(flag)
        def _(device=device):
            pl.semaphore_signal(barrier, inc=1, device_id=device, device_id_type=MESH)

    partners = ny - 1 + (one(low_a) + one(high_a)) * (1 + one(low_b) + one(high_b))

    def zero_when(flag, ref, index):
        @pl.when(jnp.logical_not(flag))
        def _():
            ref[index] = jnp.zeros(ref.at[index].shape, ref.dtype)

    inner_a, inner_b = slice(1, rows + 1), slice(1, cols + 1)
    halo_at = [
        (rows + 1, inner_b),
        (0, inner_b),
        (inner_a, cols + 1),
        (inner_a, 0),
    ]
    for d in range(4):
        zero_when(has_from[d], px, halo_at[d])
        zero_when(has_from[d], halo0, d)
        zero_when(has_from[d], lf_halo, d)
        zero_when(corner_has_from[d], lf_corner, d)

    loads[0].wait()
    stage[...] = px[inner_a, inner_b].astype(F32)[:, :, 0:8, :].reshape(faces * 8, width)
    x0[inner_a, 8 : 8 + cols] = stage[pl.ds(0, faces, stride=8), :].reshape(rows, cols, width)
    edge[0] = x0[1, 8 : 8 + cols].astype(BF)
    edge[1] = x0[rows, 8 : 8 + cols].astype(BF)
    edge[2] = stage[pl.ds(0, rows, stride=8 * cols), :].astype(BF)
    edge[3] = stage[pl.ds(8 * (cols - 1), rows, stride=8 * cols), :].astype(BF)

    def remote(src, dst, send, recv, device):
        return pltpu.make_async_remote_copy(
            src_ref=src, dst_ref=dst, send_sem=send, recv_sem=recv, device_id=device, device_id_type=MESH
        )

    layer_copies = [
        remote(edge.at[d], halo0.at[d], h0_send.at[d], h0_recv.at[d], to[d]) for d in range(4)
    ]
    x_edges = [x_hbm.at[0], x_hbm.at[rows - 1], x_hbm.at[:, 0], x_hbm.at[:, cols - 1]]
    x_halos = [
        px.at[rows + 1, pl.ds(1, cols)],
        px.at[0, pl.ds(1, cols)],
        px.at[pl.ds(1, rows), cols + 1],
        px.at[pl.ds(1, rows), 0],
    ]
    x_copies = [
        remote(x_edges[d], x_halos[d], hx_send.at[d], hx_recv.at[d], to[d]) for d in range(4)
    ]
    two = 2 * tile_b
    lf_srcs = [lf.at[pl.ds(0, two)], lf.at[pl.ds(tile_nodes - two, two)], lf_edge.at[0], lf_edge.at[1]]
    lf_dsts = [lf_halo.at[0], lf_halo.at[1], lf_halo.at[2, pl.ds(0, 2 * tile_a)], lf_halo.at[3, pl.ds(0, 2 * tile_a)]]
    lf_copies = [
        remote(lf_srcs[d], lf_dsts[d], lf_send.at[d], lf_recv.at[d], to[d]) for d in range(4)
    ]
    corner_rows = [0, tile_b - 8, tile_nodes - tile_b, tile_nodes - 8]
    corner_copies = [
        remote(lf.at[pl.ds(corner_rows[d], 8)], lf_corner.at[d], lc_send.at[d], lc_recv.at[d], corner_to[d])
        for d in range(4)
    ]

    def start_when(flag, copy):
        @pl.when(flag)
        def _():
            copy.start()

    pl.semaphore_wait(barrier, partners)
    for d in range(4):
        start_when(has_to[d], layer_copies[d])
    for d in range(4):
        start_when(has_to[d], x_copies[d])

    loads[1].wait()
    loads[2].wait()
    loads[3].wait()
    slot_id = lax.broadcasted_iota(jnp.int32, (1, slots), 1)
    nodes_out[...] = jnp.full(nodes_out.shape, -1, jnp.int32)
    for o in range(ny):
        count = live[0:1, o : o + 1]
        nodes_out[o, 0:1, 0:slots] = jnp.where(slot_id < count, tn[o : o + 1, :], -1)

    def row_copies(src, dst, send, recv, per_owner):
        sends, receives = [], []
        for k in range(1, ny):
            target, source = lax.rem(j + k, ny), lax.rem(j + ny - k, ny)
            sends.append(
                remote(src(target), dst(j), send.at[k - 1], recv.at[k - 1], (i, target))
            )
            receives.append(
                remote(src(target), dst(source), send.at[k - 1], recv.at[k - 1], (i, target))
            )
        return sends, receives

    node_sends, node_receives = row_copies(
        lambda o: nodes_out.at[o], lambda o: nodes_in.at[o], nd_send, nd_recv, 1
    )
    for copy in node_sends:
        copy.start()
    nodes_in[j] = nodes_out[j]

    lf_edge[0, 0:tile_a] = lf[pl.ds(0, tile_a, stride=tile_b), :]
    lf_edge[0, tile_a : 2 * tile_a] = lf[pl.ds(1, tile_a, stride=tile_b), :]
    lf_edge[1, 0:tile_a] = lf[pl.ds(tile_b - 2, tile_a, stride=tile_b), :]
    lf_edge[1, tile_a : 2 * tile_a] = lf[pl.ds(tile_b - 1, tile_a, stride=tile_b), :]
    for d in range(4):
        start_when(has_to[d], lf_copies[d])
    for d in range(4):
        start_when(corner_has_to[d], corner_copies[d])

    loads[4].wait()
    column = jnp.broadcast_to(sc[0:1, :].astype(F32), (128, faces)).T
    for part in range(faces // 128):
        face_id = lax.broadcasted_iota(jnp.int32, (faces, 128), 1) + 128 * part
        pick[:, 128 * part : 128 * (part + 1)] = (column == face_id.astype(F32)).astype(BF)

    loads[5].wait()

    def product(a0, na, b0, nb):
        own = px[pl.ds(a0 + 1, na), b0 + 1 : b0 + 1 + nb]
        count = na * nb
        wide = own.astype(F32).reshape(count, layers, width)
        layer = lax.broadcasted_iota(jnp.int32, wide.shape, 1)
        below = jnp.where(layer == 0, 0.0, pltpu.roll(wide, 1, 1)).astype(BF)
        above = jnp.where(layer == layers - 1, 0.0, pltpu.roll(wide, layers - 1, 1)).astype(BF)
        flat = lambda v: v.reshape(count * layers, width)
        terms = [
            own,
            below,
            above,
            px[pl.ds(a0, na), b0 + 1 : b0 + 1 + nb],
            px[pl.ds(a0 + 2, na), b0 + 1 : b0 + 1 + nb],
            px[pl.ds(a0 + 1, na), b0 : b0 + nb],
            px[pl.ds(a0 + 1, na), b0 + 2 : b0 + 2 + nb],
        ]
        lhs = jnp.concatenate([flat(t) for t in terms], axis=1)
        total = jnp.dot(lhs, cw[...].reshape(7 * width, width), preferred_element_type=F32)
        out_ref[pl.ds(a0, na), b0 : b0 + nb] = total.astype(BF).reshape(na, nb, layers, width)

    def interior(first, last):
        def body(n, carry):
            product(1 + 2 * n, 2, 1, cols - 2)
            return carry

        lax.fori_loop(first, last, body, 0)

    interior(0, early)

    for d in range(4):
        pl.when(has_from[d])(layer_copies[d].wait_recv)
    x0[rows + 1, 8 : 8 + cols] = halo0[0].astype(F32)
    x0[0, 8 : 8 + cols] = halo0[1].astype(F32)
    x0[inner_a, 8 + cols : 9 + cols] = halo0[2].astype(F32).reshape(rows, 1, width)
    x0[inner_a, 7:8] = halo0[3].astype(F32).reshape(rows, 1, width)
    basal_terms = [
        x0[inner_a, 8 : 8 + cols].reshape(faces, width),
        stage[pl.ds(1, faces, stride=8), :],
        x0[0:rows, 8 : 8 + cols].reshape(faces, width),
        x0[2 : rows + 2, 8 : 8 + cols].reshape(faces, width),
        x0[inner_a, 7 : 7 + cols].reshape(faces, width),
        x0[inner_a, 9 : 9 + cols].reshape(faces, width),
    ]
    basal_lhs = jnp.concatenate([t.astype(BF) for t in basal_terms], axis=1)
    basal_w = jnp.concatenate([cw[0], cw[2:7].reshape(5 * width, width)], axis=0)
    basal = jnp.dot(basal_lhs, basal_w, preferred_element_type=F32).astype(BF)
    picked[...] = jnp.dot(pick[...], basal, preferred_element_type=F32).astype(BF)

    def slot_rows(ref):
        return lambda o: ref.at[pl.ds(pl.multiple_of(o * slots, slots), slots)]

    block_sends, block_receives = row_copies(
        slot_rows(picked), slot_rows(received), pk_send, pk_recv, slots
    )
    for copy in block_sends:
        copy.start()
    mine = pl.ds(pl.multiple_of(j * slots, slots), slots)
    received[mine, :] = picked[mine, :]

    interior(early, (rows - 2) // 2)

    for d in range(4):
        pl.when(has_from[d])(x_copies[d].wait_recv)
    product(0, 1, 0, cols)
    product(rows - 1, 1, 0, cols)
    product(1, rows - 2, 0, 1)
    product(1, rows - 2, cols - 1, 1)

    for d in range(4):
        pl.when(has_from[d])(lf_copies[d].wait_recv)
    for d in range(4):
        pl.when(corner_has_from[d])(corner_copies[d].wait_recv)
    field[...] = jnp.zeros_like(field)
    field[2 : 2 + tile_a, 8 : 8 + tile_b] = lf[...].reshape(tile_a, tile_b, width)
    field[2 + tile_a : 4 + tile_a, 8 : 8 + tile_b] = lf_halo[0].reshape(2, tile_b, width)
    field[0:2, 8 : 8 + tile_b] = lf_halo[1].reshape(2, tile_b, width)
    for side, at in ((2, 8 + tile_b), (3, 6)):
        for c in range(2):
            field[2 : 2 + tile_a, at + c : at + c + 1] = lf_halo[
                side, c * tile_a : (c + 1) * tile_a
            ].reshape(tile_a, 1, width)
    for d, (row, col, at) in enumerate(
        [(2 + tile_a, 8 + tile_b, 0), (2 + tile_a, 7, 7), (1, 8 + tile_b, 0), (1, 7, 7)]
    ):
        field[row, col : col + 1] = lf_corner[d, at : at + 1]

    def stencil(ref, a0, na, b0, nb):
        beside = (
            ref[a0 + 1 : a0 + 1 + na, b0 : b0 + nb]
            + ref[a0 - 1 : a0 - 1 + na, b0 : b0 + nb]
            + ref[a0 : a0 + na, b0 + 1 : b0 + 1 + nb]
            + ref[a0 : a0 + na, b0 - 1 : b0 - 1 + nb]
        )
        return 1.3 * ref[a0 : a0 + na, b0 : b0 + nb] - 0.2 * beside

    first = stencil(field, 1, tile_a + 2, 7, tile_b + 2)
    row_id = lax.broadcasted_iota(jnp.int32, first.shape, 0) + i * tile_a - 1
    col_id = lax.broadcasted_iota(jnp.int32, first.shape, 1) + j * tile_b - 1
    inside = (row_id >= 0) & (row_id < nx * tile_a) & (col_id >= 0) & (col_id < ny * tile_b)
    once[:, 7 : 9 + tile_b] = jnp.where(inside, first, 0.0)
    prior = stencil(once, 1, tile_a, 8, tile_b).reshape(tile_nodes, width)
    scale = jnp.exp(lf[...])

    for copy in node_receives:
        copy.wait_recv()
    node_id = lax.broadcasted_iota(jnp.int32, (tile_nodes, slots), 0)
    onehots = [(node_id == nodes_in[o, 0:1, 0:slots]).astype(F32).astype(BF) for o in range(ny)]
    for copy in block_receives:
        copy.wait_recv()
    misfit = jnp.zeros((tile_nodes, width), F32)
    for o in range(ny):
        misfit = misfit + jnp.dot(
            onehots[o], received[o * slots : (o + 1) * slots], preferred_element_type=F32
        )
    grad_ref[...] = scale * misfit + prior

    for d in range(4):
        pl.when(has_to[d])(layer_copies[d].wait_send)
        pl.when(has_to[d])(x_copies[d].wait_send)
        pl.when(has_to[d])(lf_copies[d].wait_send)
        pl.when(corner_has_to[d])(corner_copies[d].wait_send)
    for copy in node_sends + block_sends:
        copy.wait_send()


def solution(mesh):
    nx, ny = mesh.shape["gx"], mesh.shape["gy"]

    def per_device(adjoint_trace, coupling, log_friction, send_column, live_count, target_node):
        rows, cols, layers, width = adjoint_trace.shape
        tile_a, tile_b, _ = log_friction.shape
        tile_nodes = tile_a * tile_b
        faces = rows * cols
        slots = faces // ny
        vmem = pltpu.VMEM
        dma = pltpu.SemaphoreType.DMA
        anywhere = pl.BlockSpec(memory_space=pl.ANY)
        trace_update, gradient = pl.pallas_call(
            functools.partial(kernel, nx, ny, 3),
            out_shape=(
                jax.ShapeDtypeStruct(adjoint_trace.shape, BF),
                jax.ShapeDtypeStruct((tile_nodes, width), F32),
            ),
            in_specs=[anywhere] * 6,
            out_specs=(pl.BlockSpec(memory_space=vmem), pl.BlockSpec(memory_space=vmem)),
            scratch_shapes=[
                vmem((rows + 2, cols + 2, layers, width), BF),
                vmem(coupling.shape, BF),
                vmem((tile_nodes, width), F32),
                vmem((1, faces), jnp.int32),
                vmem((1, ny), jnp.int32),
                vmem((ny, slots), jnp.int32),
                vmem((faces * 8, width), F32),
                vmem((rows + 2, cols + 16, width), F32),
                vmem((4, 16, width), BF),
                vmem((4, 16, width), BF),
                vmem((2, 2 * tile_a, width), F32),
                vmem((4, 2 * tile_b, width), F32),
                vmem((4, 8, width), F32),
                vmem((tile_a + 4, tile_b + 16, width), F32),
                vmem((tile_a + 2, tile_b + 16, width), F32),
                vmem((ny, 8, 128), jnp.int32),
                vmem((ny, 8, 128), jnp.int32),
                vmem((faces, faces), BF),
                vmem((faces, width), BF),
                vmem((faces, width), BF),
                dma((6,)),
                *[dma((4,)) for _ in range(8)],
                *[dma((ny - 1,)) for _ in range(4)],
            ],
            compiler_params=pltpu.CompilerParams(
                collective_id=0, has_side_effects=True, vmem_limit_bytes=40 * 2**20
            ),
            cost_estimate=pl.CostEstimate(
                flops=2 * 7 * faces * layers * width * width,
                bytes_accessed=4 * faces * layers * width,
                transcendentals=tile_nodes * width,
            ),
        )(
            adjoint_trace,
            coupling,
            log_friction.reshape(tile_nodes, width),
            send_column.reshape(1, faces),
            live_count.reshape(1, ny),
            target_node.reshape(ny, slots),
        )
        return trace_update, gradient.reshape(tile_a, tile_b, width)

    in_specs = (
        P("gx", "gy", None, None),
        P(),
        P("gx", "gy", None),
        P("gx", "gy", None),
        P("gx", "gy", None),
        P("gx", "gy", None, None),
    )
    out_specs = (P("gx", "gy", None, None), P("gx", "gy", None))
    return jax.shard_map(
        per_device, mesh=mesh, in_specs=in_specs, out_specs=out_specs, check_vma=False
    )
```

```python
import functools

import jax
import jax.numpy as jnp
from jax import lax
from jax.experimental import pallas as pl
from jax.experimental.pallas import tpu as pltpu
from jax.sharding import PartitionSpec as P

MESH = pl.DeviceIdType.MESH
BF, F32 = jnp.bfloat16, jnp.float32


def product(px, cw, out_ref, a0, na, b0, nb):
    layers, width = px.shape[2:]
    own = px[pl.ds(a0 + 1, na), b0 + 1 : b0 + 1 + nb]
    count = na * nb
    wide = own.astype(F32).reshape(count, layers, width)
    layer = lax.broadcasted_iota(jnp.int32, wide.shape, 1)
    below = jnp.where(layer == 0, 0.0, pltpu.roll(wide, 1, 1)).astype(BF)
    above = jnp.where(layer == layers - 1, 0.0, pltpu.roll(wide, layers - 1, 1)).astype(BF)
    flat = lambda v: v.reshape(count * layers, width)
    terms = [
        own,
        below,
        above,
        px[pl.ds(a0, na), b0 + 1 : b0 + 1 + nb],
        px[pl.ds(a0 + 2, na), b0 + 1 : b0 + 1 + nb],
        px[pl.ds(a0 + 1, na), b0 : b0 + nb],
        px[pl.ds(a0 + 1, na), b0 + 2 : b0 + 2 + nb],
    ]
    lhs = jnp.concatenate([flat(t) for t in terms], axis=1)
    total = jnp.dot(lhs, cw[...].reshape(7 * width, width), preferred_element_type=F32)
    out_ref[pl.ds(a0, na), b0 : b0 + nb] = total.astype(BF).reshape(na, nb, layers, width)


def interior(px, cw, out_ref, first, last):
    def body(n, carry):
        product(px, cw, out_ref, 1 + 2 * n, 2, 1, px.shape[1] - 4)
        return carry

    if last > first:
        lax.fori_loop(first, last, body, 0)


def finish(
    ny, late,
    inner, px, cw, scale, prior, nodes, received,
    out_hbm, grad_hbm,
    rest, grad, sem,
):
    rows, cols = inner.shape[:2]
    tile_nodes, width = scale.shape
    slots = received.shape[0] // ny
    done = 2 * late
    writes = []

    def write(src, dst):
        copy = pltpu.make_async_copy(src, dst, sem.at[len(writes)])
        copy.start()
        writes.append(copy)

    def write_part(ref, a0, na, b0, nb):
        at = (pl.ds(a0, na), pl.ds(b0, nb))
        write(ref.at[at], out_hbm.at[at])

    write_part(inner, 1, done, 1, cols - 2)

    node_id = lax.broadcasted_iota(jnp.int32, (tile_nodes, slots), 0)
    misfit = jnp.zeros((tile_nodes, width), F32)
    for o in range(ny):
        onehot = (node_id == nodes[o, 0:1, 0:slots]).astype(F32).astype(BF)
        misfit = misfit + jnp.dot(
            onehot, received[o * slots : (o + 1) * slots], preferred_element_type=F32
        )
    grad[...] = scale[...] * misfit + prior[...]
    write(grad, grad_hbm)

    if done < rows - 2:
        interior(px, cw, rest, late, (rows - 2) // 2)
        write_part(rest, 1 + done, rows - 2 - done, 1, cols - 2)
    for part in (
        (0, 1, 0, cols),
        (rows - 1, 1, 0, cols),
        (1, rows - 2, 0, 1),
        (1, rows - 2, cols - 1, 1),
    ):
        product(px, cw, rest, *part)
        write_part(rest, *part)
    for copy in writes:
        copy.wait()


def kernel(
    nx, ny, early, late,
    x_hbm, c_hbm, lf_hbm, sc_hbm, live_hbm, tn_hbm,
    out_ref, px, cw, scale, prior, nodes_in, received,
    lf, sc, live, tn,
    stage, x0, edge, halo0,
    lf_edge, lf_halo, lf_corner, field, once,
    nodes_out, pick, picked,
    local_sem, h0_send, h0_recv, hx_send, hx_recv, lf_send, lf_recv, lc_send, lc_recv,
    nd_send, nd_recv, pk_send, pk_recv,
):
    i, j = lax.axis_index("gx"), lax.axis_index("gy")
    rows, cols, layers, width = x_hbm.shape
    faces = rows * cols
    slots = faces // ny
    tile_a, tile_b = once.shape[0] - 2, cols
    tile_nodes = tile_a * tile_b
    low_a, high_a, low_b, high_b = i > 0, i < nx - 1, j > 0, j < ny - 1
    one = lambda flag: flag.astype(jnp.int32)
    up = lambda v, n: lax.rem(v + 1, n)
    down = lambda v, n: lax.rem(v + n - 1, n)
    to = [(down(i, nx), j), (up(i, nx), j), (i, down(j, ny)), (i, up(j, ny))]
    has_to = [low_a, high_a, low_b, high_b]
    has_from = [high_a, low_a, high_b, low_b]
    corner_to = [(to[a][0], to[2 + b][1]) for a in (0, 1) for b in (0, 1)]
    corner_has_to = [has_to[a] & has_to[2 + b] for a in (0, 1) for b in (0, 1)]
    corner_has_from = [has_from[a] & has_from[2 + b] for a in (0, 1) for b in (0, 1)]

    loads = [
        pltpu.make_async_copy(src, dst, local_sem.at[n])
        for n, (src, dst) in enumerate(
            [
                (x_hbm, px.at[pl.ds(1, rows), pl.ds(1, cols)]),
                (lf_hbm, lf),
                (tn_hbm, tn),
                (live_hbm, live),
                (sc_hbm, sc),
                (c_hbm, cw),
            ]
        )
    ]
    for load in loads:
        load.start()

    barrier = pltpu.get_barrier_semaphore()
    for k in range(1, ny):
        pl.semaphore_signal(barrier, inc=1, device_id=(i, lax.rem(j + k, ny)), device_id_type=MESH)
    for flag, device in list(zip(has_to[:2], to[:2])) + list(zip(corner_has_to, corner_to)):

        @pl.when(flag)
        def _(device=device):
            pl.semaphore_signal(barrier, inc=1, device_id=device, device_id_type=MESH)

    partners = ny - 1 + (one(low_a) + one(high_a)) * (1 + one(low_b) + one(high_b))

    def zero_when(flag, ref, index):
        @pl.when(jnp.logical_not(flag))
        def _():
            ref[index] = jnp.zeros(ref.at[index].shape, ref.dtype)

    inner_a, inner_b = slice(1, rows + 1), slice(1, cols + 1)
    halo_at = [
        (rows + 1, inner_b),
        (0, inner_b),
        (inner_a, cols + 1),
        (inner_a, 0),
    ]
    for d in range(4):
        zero_when(has_from[d], px, halo_at[d])
        zero_when(has_from[d], halo0, d)
        zero_when(has_from[d], lf_halo, d)
        zero_when(corner_has_from[d], lf_corner, d)

    loads[0].wait()
    stage[...] = px[inner_a, inner_b].astype(F32)[:, :, 0:8, :].reshape(faces * 8, width)
    x0[inner_a, 8 : 8 + cols] = stage[pl.ds(0, faces, stride=8), :].reshape(rows, cols, width)
    edge[0] = x0[1, 8 : 8 + cols].astype(BF)
    edge[1] = x0[rows, 8 : 8 + cols].astype(BF)
    edge[2] = stage[pl.ds(0, rows, stride=8 * cols), :].astype(BF)
    edge[3] = stage[pl.ds(8 * (cols - 1), rows, stride=8 * cols), :].astype(BF)

    def remote(src, dst, send, recv, device):
        return pltpu.make_async_remote_copy(
            src_ref=src, dst_ref=dst, send_sem=send, recv_sem=recv, device_id=device, device_id_type=MESH
        )

    layer_copies = [
        remote(edge.at[d], halo0.at[d], h0_send.at[d], h0_recv.at[d], to[d]) for d in range(4)
    ]
    x_edges = [x_hbm.at[0], x_hbm.at[rows - 1], x_hbm.at[:, 0], x_hbm.at[:, cols - 1]]
    x_halos = [
        px.at[rows + 1, pl.ds(1, cols)],
        px.at[0, pl.ds(1, cols)],
        px.at[pl.ds(1, rows), cols + 1],
        px.at[pl.ds(1, rows), 0],
    ]
    x_copies = [
        remote(x_edges[d], x_halos[d], hx_send.at[d], hx_recv.at[d], to[d]) for d in range(4)
    ]
    two = 2 * tile_b
    lf_srcs = [lf.at[pl.ds(0, two)], lf.at[pl.ds(tile_nodes - two, two)], lf_edge.at[0], lf_edge.at[1]]
    lf_dsts = [lf_halo.at[0], lf_halo.at[1], lf_halo.at[2, pl.ds(0, 2 * tile_a)], lf_halo.at[3, pl.ds(0, 2 * tile_a)]]
    lf_copies = [
        remote(lf_srcs[d], lf_dsts[d], lf_send.at[d], lf_recv.at[d], to[d]) for d in range(4)
    ]
    corner_rows = [0, tile_b - 8, tile_nodes - tile_b, tile_nodes - 8]
    corner_copies = [
        remote(lf.at[pl.ds(corner_rows[d], 8)], lf_corner.at[d], lc_send.at[d], lc_recv.at[d], corner_to[d])
        for d in range(4)
    ]

    def start_when(flag, copy):
        @pl.when(flag)
        def _():
            copy.start()

    pl.semaphore_wait(barrier, partners)
    for d in range(4):
        start_when(has_to[d], layer_copies[d])
    for d in range(4):
        start_when(has_to[d], x_copies[d])

    loads[1].wait()
    loads[2].wait()
    loads[3].wait()
    slot_id = lax.broadcasted_iota(jnp.int32, (1, slots), 1)
    nodes_out[...] = jnp.full(nodes_out.shape, -1, jnp.int32)
    for o in range(ny):
        count = live[0:1, o : o + 1]
        nodes_out[o, 0:1, 0:slots] = jnp.where(slot_id < count, tn[o : o + 1, :], -1)

    def row_copies(src, dst, send, recv, per_owner):
        sends, receives = [], []
        for k in range(1, ny):
            target, source = lax.rem(j + k, ny), lax.rem(j + ny - k, ny)
            sends.append(
                remote(src(target), dst(j), send.at[k - 1], recv.at[k - 1], (i, target))
            )
            receives.append(
                remote(src(target), dst(source), send.at[k - 1], recv.at[k - 1], (i, target))
            )
        return sends, receives

    node_sends, node_receives = row_copies(
        lambda o: nodes_out.at[o], lambda o: nodes_in.at[o], nd_send, nd_recv, 1
    )
    for copy in node_sends:
        copy.start()
    nodes_in[j] = nodes_out[j]

    lf_edge[0, 0:tile_a] = lf[pl.ds(0, tile_a, stride=tile_b), :]
    lf_edge[0, tile_a : 2 * tile_a] = lf[pl.ds(1, tile_a, stride=tile_b), :]
    lf_edge[1, 0:tile_a] = lf[pl.ds(tile_b - 2, tile_a, stride=tile_b), :]
    lf_edge[1, tile_a : 2 * tile_a] = lf[pl.ds(tile_b - 1, tile_a, stride=tile_b), :]
    for d in range(4):
        start_when(has_to[d], lf_copies[d])
    for d in range(4):
        start_when(corner_has_to[d], corner_copies[d])

    loads[4].wait()
    column = jnp.broadcast_to(sc[0:1, :].astype(F32), (128, faces)).T
    for part in range(faces // 128):
        face_id = lax.broadcasted_iota(jnp.int32, (faces, 128), 1) + 128 * part
        pick[:, 128 * part : 128 * (part + 1)] = (column == face_id.astype(F32)).astype(BF)

    loads[5].wait()

    interior(px, cw, out_ref, 0, early)

    for d in range(4):
        pl.when(has_from[d])(layer_copies[d].wait_recv)
    x0[rows + 1, 8 : 8 + cols] = halo0[0].astype(F32)
    x0[0, 8 : 8 + cols] = halo0[1].astype(F32)
    x0[inner_a, 8 + cols : 9 + cols] = halo0[2].astype(F32).reshape(rows, 1, width)
    x0[inner_a, 7:8] = halo0[3].astype(F32).reshape(rows, 1, width)
    basal_terms = [
        x0[inner_a, 8 : 8 + cols].reshape(faces, width),
        stage[pl.ds(1, faces, stride=8), :],
        x0[0:rows, 8 : 8 + cols].reshape(faces, width),
        x0[2 : rows + 2, 8 : 8 + cols].reshape(faces, width),
        x0[inner_a, 7 : 7 + cols].reshape(faces, width),
        x0[inner_a, 9 : 9 + cols].reshape(faces, width),
    ]
    basal_lhs = jnp.concatenate([t.astype(BF) for t in basal_terms], axis=1)
    basal_w = jnp.concatenate([cw[0], cw[2:7].reshape(5 * width, width)], axis=0)
    basal = jnp.dot(basal_lhs, basal_w, preferred_element_type=F32).astype(BF)
    picked[...] = jnp.dot(pick[...], basal, preferred_element_type=F32).astype(BF)

    def slot_rows(ref):
        return lambda o: ref.at[pl.ds(pl.multiple_of(o * slots, slots), slots)]

    block_sends, block_receives = row_copies(
        slot_rows(picked), slot_rows(received), pk_send, pk_recv, slots
    )
    for copy in block_sends:
        copy.start()
    mine = pl.ds(pl.multiple_of(j * slots, slots), slots)
    received[mine, :] = picked[mine, :]

    interior(px, cw, out_ref, early, late)

    for d in range(4):
        pl.when(has_from[d])(lf_copies[d].wait_recv)
    for d in range(4):
        pl.when(corner_has_from[d])(corner_copies[d].wait_recv)
    field[...] = jnp.zeros_like(field)
    field[2 : 2 + tile_a, 8 : 8 + tile_b] = lf[...].reshape(tile_a, tile_b, width)
    field[2 + tile_a : 4 + tile_a, 8 : 8 + tile_b] = lf_halo[0].reshape(2, tile_b, width)
    field[0:2, 8 : 8 + tile_b] = lf_halo[1].reshape(2, tile_b, width)
    for side, at in ((2, 8 + tile_b), (3, 6)):
        for c in range(2):
            field[2 : 2 + tile_a, at + c : at + c + 1] = lf_halo[
                side, c * tile_a : (c + 1) * tile_a
            ].reshape(tile_a, 1, width)
    for d, (row, col, at) in enumerate(
        [(2 + tile_a, 8 + tile_b, 0), (2 + tile_a, 7, 7), (1, 8 + tile_b, 0), (1, 7, 7)]
    ):
        field[row, col : col + 1] = lf_corner[d, at : at + 1]

    def stencil(ref, a0, na, b0, nb):
        beside = (
            ref[a0 + 1 : a0 + 1 + na, b0 : b0 + nb]
            + ref[a0 - 1 : a0 - 1 + na, b0 : b0 + nb]
            + ref[a0 : a0 + na, b0 + 1 : b0 + 1 + nb]
            + ref[a0 : a0 + na, b0 - 1 : b0 - 1 + nb]
        )
        return 1.3 * ref[a0 : a0 + na, b0 : b0 + nb] - 0.2 * beside

    first = stencil(field, 1, tile_a + 2, 7, tile_b + 2)
    row_id = lax.broadcasted_iota(jnp.int32, first.shape, 0) + i * tile_a - 1
    col_id = lax.broadcasted_iota(jnp.int32, first.shape, 1) + j * tile_b - 1
    inside = (row_id >= 0) & (row_id < nx * tile_a) & (col_id >= 0) & (col_id < ny * tile_b)
    once[:, 7 : 9 + tile_b] = jnp.where(inside, first, 0.0)
    prior[...] = stencil(once, 1, tile_a, 8, tile_b).reshape(tile_nodes, width)
    scale[...] = jnp.exp(lf[...])

    for d in range(4):
        pl.when(has_from[d])(x_copies[d].wait_recv)
    for copy in node_receives + block_receives:
        copy.wait_recv()
    for d in range(4):
        pl.when(has_to[d])(layer_copies[d].wait_send)
        pl.when(has_to[d])(x_copies[d].wait_send)
        pl.when(has_to[d])(lf_copies[d].wait_send)
        pl.when(corner_has_to[d])(corner_copies[d].wait_send)
    for copy in node_sends + block_sends:
        copy.wait_send()


def solution(mesh):
    nx, ny = mesh.shape["gx"], mesh.shape["gy"]

    def per_device(adjoint_trace, coupling, log_friction, send_column, live_count, target_node):
        rows, cols, layers, width = adjoint_trace.shape
        tile_a, tile_b, _ = log_friction.shape
        tile_nodes = tile_a * tile_b
        faces = rows * cols
        slots = faces // ny
        vmem = pltpu.VMEM
        dma = pltpu.SemaphoreType.DMA
        hbm = pl.BlockSpec(memory_space=pltpu.HBM)
        local = pl.BlockSpec(memory_space=vmem)
        shape = jax.ShapeDtypeStruct
        early, late = 3, (rows - 2) // 2
        held = pl.pallas_call(
            functools.partial(kernel, nx, ny, early, late),
            out_shape=(
                shape(adjoint_trace.shape, BF),
                shape((rows + 2, cols + 2, layers, width), BF),
                shape(coupling.shape, BF),
                shape((tile_nodes, width), F32),
                shape((tile_nodes, width), F32),
                shape((ny, 8, 128), jnp.int32),
                shape((faces, width), BF),
            ),
            in_specs=[hbm] * 6,
            out_specs=(local,) * 7,
            scratch_shapes=[
                vmem((tile_nodes, width), F32),
                vmem((1, faces), jnp.int32),
                vmem((1, ny), jnp.int32),
                vmem((ny, slots), jnp.int32),
                vmem((faces * 8, width), F32),
                vmem((rows + 2, cols + 16, width), F32),
                vmem((4, 16, width), BF),
                vmem((4, 16, width), BF),
                vmem((2, 2 * tile_a, width), F32),
                vmem((4, 2 * tile_b, width), F32),
                vmem((4, 8, width), F32),
                vmem((tile_a + 4, tile_b + 16, width), F32),
                vmem((tile_a + 2, tile_b + 16, width), F32),
                vmem((ny, 8, 128), jnp.int32),
                vmem((faces, faces), BF),
                vmem((faces, width), BF),
                dma((6,)),
                *[dma((4,)) for _ in range(8)],
                *[dma((ny - 1,)) for _ in range(4)],
            ],
            compiler_params=pltpu.CompilerParams(
                collective_id=0, has_side_effects=True, vmem_limit_bytes=24 * 2**20
            ),
            cost_estimate=pl.CostEstimate(
                flops=2 * 7 * faces * layers * width * width,
                bytes_accessed=4 * faces * layers * width,
                transcendentals=tile_nodes * width,
            ),
        )(
            *[
                pltpu.with_memory_space_constraint(operand, pltpu.HBM)
                for operand in (
                    adjoint_trace,
                    coupling,
                    log_friction.reshape(tile_nodes, width),
                    send_column.reshape(1, faces),
                    live_count.reshape(1, ny),
                    target_node.reshape(ny, slots),
                )
            ]
        )
        trace_update, gradient = pl.pallas_call(
            functools.partial(finish, ny, late),
            out_shape=(shape(adjoint_trace.shape, BF), shape((tile_nodes, width), F32)),
            in_specs=[local] * 7,
            out_specs=(hbm, hbm),
            scratch_shapes=[
                vmem(adjoint_trace.shape, BF),
                vmem((tile_nodes, width), F32),
                dma((8,)),
            ],
            compiler_params=pltpu.CompilerParams(vmem_limit_bytes=24 * 2**20),
        )(*held)
        return trace_update, gradient.reshape(tile_a, tile_b, width)

    in_specs = (
        P("gx", "gy", None, None),
        P(),
        P("gx", "gy", None),
        P("gx", "gy", None),
        P("gx", "gy", None),
        P("gx", "gy", None, None),
    )
    out_specs = (P("gx", "gy", None, None), P("gx", "gy", None))
    return jax.shard_map(
        per_device, mesh=mesh, in_specs=in_specs, out_specs=out_specs, check_vma=False
    )
```

```python
import functools

import jax
import jax.numpy as jnp
from jax import lax
from jax.experimental import pallas as pl
from jax.experimental.pallas import tpu as pltpu
from jax.sharding import PartitionSpec as P

MESH = pl.DeviceIdType.MESH
BF, F32 = jnp.bfloat16, jnp.float32


def product(px, cw, out_ref, a0, na, b0, nb):
    layers, width = px.shape[2:]
    own = px[pl.ds(a0 + 1, na), b0 + 1 : b0 + 1 + nb]
    count = na * nb
    wide = own.astype(F32).reshape(count, layers, width)
    layer = lax.broadcasted_iota(jnp.int32, wide.shape, 1)
    below = jnp.where(layer == 0, 0.0, pltpu.roll(wide, 1, 1)).astype(BF)
    above = jnp.where(layer == layers - 1, 0.0, pltpu.roll(wide, layers - 1, 1)).astype(BF)
    flat = lambda v: v.reshape(count * layers, width)
    terms = [
        own,
        below,
        above,
        px[pl.ds(a0, na), b0 + 1 : b0 + 1 + nb],
        px[pl.ds(a0 + 2, na), b0 + 1 : b0 + 1 + nb],
        px[pl.ds(a0 + 1, na), b0 : b0 + nb],
        px[pl.ds(a0 + 1, na), b0 + 2 : b0 + 2 + nb],
    ]
    lhs = jnp.concatenate([flat(t) for t in terms], axis=1)
    total = jnp.dot(lhs, cw[...].reshape(7 * width, width), preferred_element_type=F32)
    out_ref[pl.ds(a0, na), b0 : b0 + nb] = total.astype(BF).reshape(na, nb, layers, width)


def interior(px, cw, out_ref, first, last):
    def body(n, carry):
        product(px, cw, out_ref, 1 + 2 * n, 2, 1, px.shape[1] - 4)
        return carry

    if last > first:
        lax.fori_loop(first, last, body, 0)


def finish(
    ny, late,
    inner, px, cw, scale, prior, nodes, received,
    out_hbm, grad_hbm,
    rest, grad, sem,
):
    rows, cols = inner.shape[:2]
    tile_nodes, width = scale.shape
    slots = received.shape[0] // ny
    done = 2 * late
    writes = []

    def write(src, dst):
        copy = pltpu.make_async_copy(src, dst, sem.at[len(writes)])
        copy.start()
        writes.append(copy)

    def write_part(ref, a0, na, b0, nb):
        at = (pl.ds(a0, na), pl.ds(b0, nb))
        write(ref.at[at], out_hbm.at[at])

    write_part(inner, 1, done, 1, cols - 2)

    node_id = lax.broadcasted_iota(jnp.int32, (tile_nodes, slots), 0)
    misfit = jnp.zeros((tile_nodes, width), F32)
    for o in range(ny):
        onehot = (node_id == nodes[o, 0:1, 0:slots]).astype(F32).astype(BF)
        misfit = misfit + jnp.dot(
            onehot, received[o * slots : (o + 1) * slots], preferred_element_type=F32
        )
    grad[...] = scale[...] * misfit + prior[...]
    write(grad, grad_hbm)

    if done < rows - 2:
        interior(px, cw, rest, late, (rows - 2) // 2)
        write_part(rest, 1 + done, rows - 2 - done, 1, cols - 2)
    for part in (
        (0, 1, 0, cols),
        (rows - 1, 1, 0, cols),
        (1, rows - 2, 0, 1),
        (1, rows - 2, cols - 1, 1),
    ):
        product(px, cw, rest, *part)
        write_part(rest, *part)
    for copy in writes:
        copy.wait()


def kernel(
    nx, ny, early, late,
    x_hbm, c_hbm, lf_hbm, sc_hbm, live_hbm, tn_hbm,
    out_ref, px, cw, scale, prior, nodes_in, received,
    lf, sc, live, tn,
    stage, x0, edge, halo0,
    lf_edge, lf_halo, lf_corner, field, once,
    nodes_out, pick, picked,
    local_sem, h0_send, h0_recv, hx_send, hx_recv, lf_send, lf_recv, lc_send, lc_recv,
    nd_send, nd_recv, pk_send, pk_recv,
):
    i, j = lax.axis_index("gx"), lax.axis_index("gy")
    rows, cols, layers, width = x_hbm.shape
    faces = rows * cols
    slots = faces // ny
    tile_a, tile_b = once.shape[0] - 2, cols
    tile_nodes = tile_a * tile_b
    low_a, high_a, low_b, high_b = i > 0, i < nx - 1, j > 0, j < ny - 1
    one = lambda flag: flag.astype(jnp.int32)
    up = lambda v, n: lax.rem(v + 1, n)
    down = lambda v, n: lax.rem(v + n - 1, n)
    to = [(down(i, nx), j), (up(i, nx), j), (i, down(j, ny)), (i, up(j, ny))]
    has_to = [low_a, high_a, low_b, high_b]
    has_from = [high_a, low_a, high_b, low_b]
    corner_to = [(to[a][0], to[2 + b][1]) for a in (0, 1) for b in (0, 1)]
    corner_has_to = [has_to[a] & has_to[2 + b] for a in (0, 1) for b in (0, 1)]
    corner_has_from = [has_from[a] & has_from[2 + b] for a in (0, 1) for b in (0, 1)]

    loads = [
        pltpu.make_async_copy(src, dst, local_sem.at[n])
        for n, (src, dst) in enumerate(
            [
                (x_hbm, px.at[pl.ds(1, rows), pl.ds(1, cols)]),
                (lf_hbm, lf),
                (tn_hbm, tn),
                (live_hbm, live),
                (sc_hbm, sc),
                (c_hbm, cw),
            ]
        )
    ]
    barrier = pltpu.get_barrier_semaphore()
    for k in range(1, ny):
        pl.semaphore_signal(barrier, inc=1, device_id=(i, lax.rem(j + k, ny)), device_id_type=MESH)
    for flag, device in list(zip(has_to[:2], to[:2])) + list(zip(corner_has_to, corner_to)):

        @pl.when(flag)
        def _(device=device):
            pl.semaphore_signal(barrier, inc=1, device_id=device, device_id_type=MESH)

    for load in loads:
        load.start()

    partners = ny - 1 + (one(low_a) + one(high_a)) * (1 + one(low_b) + one(high_b))

    def zero_when(flag, ref, index):
        @pl.when(jnp.logical_not(flag))
        def _():
            ref[index] = jnp.zeros(ref.at[index].shape, ref.dtype)

    inner_a, inner_b = slice(1, rows + 1), slice(1, cols + 1)
    halo_at = [
        (rows + 1, inner_b),
        (0, inner_b),
        (inner_a, cols + 1),
        (inner_a, 0),
    ]
    for d in range(4):
        zero_when(has_from[d], px, halo_at[d])
        zero_when(has_from[d], halo0, d)
        zero_when(has_from[d], lf_halo, d)
        zero_when(corner_has_from[d], lf_corner, d)

    def remote(src, dst, send, recv, device):
        return pltpu.make_async_remote_copy(
            src_ref=src, dst_ref=dst, send_sem=send, recv_sem=recv, device_id=device, device_id_type=MESH
        )

    x_edges = [x_hbm.at[0], x_hbm.at[rows - 1], x_hbm.at[:, 0], x_hbm.at[:, cols - 1]]
    x_halos = [
        px.at[rows + 1, pl.ds(1, cols)],
        px.at[0, pl.ds(1, cols)],
        px.at[pl.ds(1, rows), cols + 1],
        px.at[pl.ds(1, rows), 0],
    ]
    x_copies = [
        remote(x_edges[d], x_halos[d], hx_send.at[d], hx_recv.at[d], to[d]) for d in range(4)
    ]
    def start_when(flag, copy):
        @pl.when(flag)
        def _():
            copy.start()

    pl.semaphore_wait(barrier, partners)
    for d in range(4):
        start_when(has_to[d], x_copies[d])

    loads[0].wait()
    stage[...] = px[inner_a, inner_b].astype(F32)[:, :, 0:8, :].reshape(faces * 8, width)
    x0[inner_a, 8 : 8 + cols] = stage[pl.ds(0, faces, stride=8), :].reshape(rows, cols, width)
    edge[0] = x0[1, 8 : 8 + cols].astype(BF)
    edge[1] = x0[rows, 8 : 8 + cols].astype(BF)
    edge[2] = stage[pl.ds(0, rows, stride=8 * cols), :].astype(BF)
    edge[3] = stage[pl.ds(8 * (cols - 1), rows, stride=8 * cols), :].astype(BF)

    layer_copies = [
        remote(edge.at[d], halo0.at[d], h0_send.at[d], h0_recv.at[d], to[d]) for d in range(4)
    ]
    two = 2 * tile_b
    lf_srcs = [lf.at[pl.ds(0, two)], lf.at[pl.ds(tile_nodes - two, two)], lf_edge.at[0], lf_edge.at[1]]
    lf_dsts = [lf_halo.at[0], lf_halo.at[1], lf_halo.at[2, pl.ds(0, 2 * tile_a)], lf_halo.at[3, pl.ds(0, 2 * tile_a)]]
    lf_copies = [
        remote(lf_srcs[d], lf_dsts[d], lf_send.at[d], lf_recv.at[d], to[d]) for d in range(4)
    ]
    corner_rows = [0, tile_b - 8, tile_nodes - tile_b, tile_nodes - 8]
    corner_copies = [
        remote(lf.at[pl.ds(corner_rows[d], 8)], lf_corner.at[d], lc_send.at[d], lc_recv.at[d], corner_to[d])
        for d in range(4)
    ]

    for d in range(4):
        start_when(has_to[d], layer_copies[d])

    loads[1].wait()
    loads[2].wait()
    loads[3].wait()
    slot_id = lax.broadcasted_iota(jnp.int32, (1, slots), 1)
    nodes_out[...] = jnp.full(nodes_out.shape, -1, jnp.int32)
    for o in range(ny):
        count = live[0:1, o : o + 1]
        nodes_out[o, 0:1, 0:slots] = jnp.where(slot_id < count, tn[o : o + 1, :], -1)

    def row_copies(src, dst, send, recv, per_owner):
        sends, receives = [], []
        for k in range(1, ny):
            target, source = lax.rem(j + k, ny), lax.rem(j + ny - k, ny)
            sends.append(
                remote(src(target), dst(j), send.at[k - 1], recv.at[k - 1], (i, target))
            )
            receives.append(
                remote(src(target), dst(source), send.at[k - 1], recv.at[k - 1], (i, target))
            )
        return sends, receives

    node_sends, node_receives = row_copies(
        lambda o: nodes_out.at[o], lambda o: nodes_in.at[o], nd_send, nd_recv, 1
    )
    for copy in node_sends:
        copy.start()
    nodes_in[j] = nodes_out[j]

    lf_edge[0, 0:tile_a] = lf[pl.ds(0, tile_a, stride=tile_b), :]
    lf_edge[0, tile_a : 2 * tile_a] = lf[pl.ds(1, tile_a, stride=tile_b), :]
    lf_edge[1, 0:tile_a] = lf[pl.ds(tile_b - 2, tile_a, stride=tile_b), :]
    lf_edge[1, tile_a : 2 * tile_a] = lf[pl.ds(tile_b - 1, tile_a, stride=tile_b), :]
    for d in range(4):
        start_when(has_to[d], lf_copies[d])
    for d in range(4):
        start_when(corner_has_to[d], corner_copies[d])

    loads[4].wait()
    column = jnp.broadcast_to(sc[0:1, :].astype(F32), (128, faces)).T
    for part in range(faces // 128):
        face_id = lax.broadcasted_iota(jnp.int32, (faces, 128), 1) + 128 * part
        pick[:, 128 * part : 128 * (part + 1)] = (column == face_id.astype(F32)).astype(BF)

    loads[5].wait()

    interior(px, cw, out_ref, 0, early)

    for d in range(4):
        pl.when(has_from[d])(layer_copies[d].wait_recv)
    x0[rows + 1, 8 : 8 + cols] = halo0[0].astype(F32)
    x0[0, 8 : 8 + cols] = halo0[1].astype(F32)
    x0[inner_a, 8 + cols : 9 + cols] = halo0[2].astype(F32).reshape(rows, 1, width)
    x0[inner_a, 7:8] = halo0[3].astype(F32).reshape(rows, 1, width)
    basal_terms = [
        x0[inner_a, 8 : 8 + cols].reshape(faces, width),
        stage[pl.ds(1, faces, stride=8), :],
        x0[0:rows, 8 : 8 + cols].reshape(faces, width),
        x0[2 : rows + 2, 8 : 8 + cols].reshape(faces, width),
        x0[inner_a, 7 : 7 + cols].reshape(faces, width),
        x0[inner_a, 9 : 9 + cols].reshape(faces, width),
    ]
    basal_lhs = jnp.concatenate([t.astype(BF) for t in basal_terms], axis=1)
    basal_w = jnp.concatenate([cw[0], cw[2:7].reshape(5 * width, width)], axis=0)
    basal = jnp.dot(basal_lhs, basal_w, preferred_element_type=F32).astype(BF)
    picked[...] = jnp.dot(pick[...], basal, preferred_element_type=F32).astype(BF)

    def slot_rows(ref):
        return lambda o: ref.at[pl.ds(pl.multiple_of(o * slots, slots), slots)]

    block_sends, block_receives = row_copies(
        slot_rows(picked), slot_rows(received), pk_send, pk_recv, slots
    )
    for copy in block_sends:
        copy.start()
    mine = pl.ds(pl.multiple_of(j * slots, slots), slots)
    received[mine, :] = picked[mine, :]

    interior(px, cw, out_ref, early, late)

    for d in range(4):
        pl.when(has_from[d])(lf_copies[d].wait_recv)
    for d in range(4):
        pl.when(corner_has_from[d])(corner_copies[d].wait_recv)
    field[...] = jnp.zeros_like(field)
    field[2 : 2 + tile_a, 8 : 8 + tile_b] = lf[...].reshape(tile_a, tile_b, width)
    field[2 + tile_a : 4 + tile_a, 8 : 8 + tile_b] = lf_halo[0].reshape(2, tile_b, width)
    field[0:2, 8 : 8 + tile_b] = lf_halo[1].reshape(2, tile_b, width)
    for side, at in ((2, 8 + tile_b), (3, 6)):
        for c in range(2):
            field[2 : 2 + tile_a, at + c : at + c + 1] = lf_halo[
                side, c * tile_a : (c + 1) * tile_a
            ].reshape(tile_a, 1, width)
    for d, (row, col, at) in enumerate(
        [(2 + tile_a, 8 + tile_b, 0), (2 + tile_a, 7, 7), (1, 8 + tile_b, 0), (1, 7, 7)]
    ):
        field[row, col : col + 1] = lf_corner[d, at : at + 1]

    def stencil(ref, a0, na, b0, nb):
        beside = (
            ref[a0 + 1 : a0 + 1 + na, b0 : b0 + nb]
            + ref[a0 - 1 : a0 - 1 + na, b0 : b0 + nb]
            + ref[a0 : a0 + na, b0 + 1 : b0 + 1 + nb]
            + ref[a0 : a0 + na, b0 - 1 : b0 - 1 + nb]
        )
        return 1.3 * ref[a0 : a0 + na, b0 : b0 + nb] - 0.2 * beside

    first = stencil(field, 1, tile_a + 2, 7, tile_b + 2)
    row_id = lax.broadcasted_iota(jnp.int32, first.shape, 0) + i * tile_a - 1
    col_id = lax.broadcasted_iota(jnp.int32, first.shape, 1) + j * tile_b - 1
    inside = (row_id >= 0) & (row_id < nx * tile_a) & (col_id >= 0) & (col_id < ny * tile_b)
    once[:, 7 : 9 + tile_b] = jnp.where(inside, first, 0.0)
    prior[...] = stencil(once, 1, tile_a, 8, tile_b).reshape(tile_nodes, width)
    scale[...] = jnp.exp(lf[...])

    for d in range(4):
        pl.when(has_from[d])(x_copies[d].wait_recv)
    for copy in node_receives + block_receives:
        copy.wait_recv()
    for d in range(4):
        pl.when(has_to[d])(layer_copies[d].wait_send)
        pl.when(has_to[d])(x_copies[d].wait_send)
        pl.when(has_to[d])(lf_copies[d].wait_send)
        pl.when(corner_has_to[d])(corner_copies[d].wait_send)
    for copy in node_sends + block_sends:
        copy.wait_send()


def solution(mesh):
    nx, ny = mesh.shape["gx"], mesh.shape["gy"]

    def per_device(adjoint_trace, coupling, log_friction, send_column, live_count, target_node):
        rows, cols, layers, width = adjoint_trace.shape
        tile_a, tile_b, _ = log_friction.shape
        tile_nodes = tile_a * tile_b
        faces = rows * cols
        slots = faces // ny
        vmem = pltpu.VMEM
        dma = pltpu.SemaphoreType.DMA
        hbm = pl.BlockSpec(memory_space=pltpu.HBM)
        local = pl.BlockSpec(memory_space=vmem)
        shape = jax.ShapeDtypeStruct
        early, late = 3, (rows - 2) // 2
        held = pl.pallas_call(
            functools.partial(kernel, nx, ny, early, late),
            out_shape=(
                shape(adjoint_trace.shape, BF),
                shape((rows + 2, cols + 2, layers, width), BF),
                shape(coupling.shape, BF),
                shape((tile_nodes, width), F32),
                shape((tile_nodes, width), F32),
                shape((ny, 8, 128), jnp.int32),
                shape((faces, width), BF),
            ),
            in_specs=[hbm] * 6,
            out_specs=(local,) * 7,
            scratch_shapes=[
                vmem((tile_nodes, width), F32),
                vmem((1, faces), jnp.int32),
                vmem((1, ny), jnp.int32),
                vmem((ny, slots), jnp.int32),
                vmem((faces * 8, width), F32),
                vmem((rows + 2, cols + 16, width), F32),
                vmem((4, 16, width), BF),
                vmem((4, 16, width), BF),
                vmem((2, 2 * tile_a, width), F32),
                vmem((4, 2 * tile_b, width), F32),
                vmem((4, 8, width), F32),
                vmem((tile_a + 4, tile_b + 16, width), F32),
                vmem((tile_a + 2, tile_b + 16, width), F32),
                vmem((ny, 8, 128), jnp.int32),
                vmem((faces, faces), BF),
                vmem((faces, width), BF),
                dma((6,)),
                *[dma((4,)) for _ in range(8)],
                *[dma((ny - 1,)) for _ in range(4)],
            ],
            compiler_params=pltpu.CompilerParams(
                collective_id=0, has_side_effects=True, vmem_limit_bytes=24 * 2**20
            ),
            cost_estimate=pl.CostEstimate(
                flops=2 * 7 * faces * layers * width * width,
                bytes_accessed=4 * faces * layers * width,
                transcendentals=tile_nodes * width,
            ),
        )(
            *[
                pltpu.with_memory_space_constraint(operand, pltpu.HBM)
                for operand in (
                    adjoint_trace,
                    coupling,
                    log_friction.reshape(tile_nodes, width),
                    send_column.reshape(1, faces),
                    live_count.reshape(1, ny),
                    target_node.reshape(ny, slots),
                )
            ]
        )
        trace_update, gradient = pl.pallas_call(
            functools.partial(finish, ny, late),
            out_shape=(shape(adjoint_trace.shape, BF), shape((tile_nodes, width), F32)),
            in_specs=[local] * 7,
            out_specs=(hbm, hbm),
            scratch_shapes=[
                vmem(adjoint_trace.shape, BF),
                vmem((tile_nodes, width), F32),
                dma((8,)),
            ],
            compiler_params=pltpu.CompilerParams(vmem_limit_bytes=24 * 2**20),
        )(*held)
        return trace_update, gradient.reshape(tile_a, tile_b, width)

    in_specs = (
        P("gx", "gy", None, None),
        P(),
        P("gx", "gy", None),
        P("gx", "gy", None),
        P("gx", "gy", None),
        P("gx", "gy", None, None),
    )
    out_specs = (P("gx", "gy", None, None), P("gx", "gy", None))
    return jax.shard_map(
        per_device, mesh=mesh, in_specs=in_specs, out_specs=out_specs, check_vma=False
    )
```

```python
import functools

import jax
import jax.numpy as jnp
from jax import lax
from jax.experimental import pallas as pl
from jax.experimental.pallas import tpu as pltpu
from jax.sharding import PartitionSpec as P

MESH = pl.DeviceIdType.MESH
BF, F32 = jnp.bfloat16, jnp.float32


def product(px, cw, out_ref, a0, na, b0, nb):
    layers, width = px.shape[2:]
    own = px[pl.ds(a0 + 1, na), b0 + 1 : b0 + 1 + nb]
    count = na * nb
    wide = own.astype(F32).reshape(count, layers, width)
    layer = lax.broadcasted_iota(jnp.int32, wide.shape, 1)
    below = jnp.where(layer == 0, 0.0, pltpu.roll(wide, 1, 1)).astype(BF)
    above = jnp.where(layer == layers - 1, 0.0, pltpu.roll(wide, layers - 1, 1)).astype(BF)
    flat = lambda v: v.reshape(count * layers, width)
    terms = [
        own,
        below,
        above,
        px[pl.ds(a0, na), b0 + 1 : b0 + 1 + nb],
        px[pl.ds(a0 + 2, na), b0 + 1 : b0 + 1 + nb],
        px[pl.ds(a0 + 1, na), b0 : b0 + nb],
        px[pl.ds(a0 + 1, na), b0 + 2 : b0 + 2 + nb],
    ]
    lhs = jnp.concatenate([flat(t) for t in terms], axis=1)
    total = jnp.dot(lhs, cw[...].reshape(7 * width, width), preferred_element_type=F32)
    out_ref[pl.ds(a0, na), b0 : b0 + nb] = total.astype(BF).reshape(na, nb, layers, width)


def interior(px, cw, out_ref, first, last):
    def body(n, carry):
        product(px, cw, out_ref, 1 + 2 * n, 2, 1, px.shape[1] - 4)
        return carry

    if last > first:
        lax.fori_loop(first, last, body, 0)


def finish(
    ny, late,
    inner, px, cw, scale, prior, nodes, received,
    out_hbm, grad_hbm,
    rest, grad, sem,
):
    rows, cols = inner.shape[:2]
    tile_nodes, width = scale.shape
    slots = received.shape[0] // ny
    done = 2 * late
    writes = []

    def write(src, dst):
        copy = pltpu.make_async_copy(src, dst, sem.at[len(writes)])
        copy.start()
        writes.append(copy)

    def write_part(ref, a0, na, b0, nb):
        at = (pl.ds(a0, na), pl.ds(b0, nb))
        write(ref.at[at], out_hbm.at[at])

    write_part(inner, 1, done, 1, cols - 2)

    node_id = lax.broadcasted_iota(jnp.int32, (tile_nodes, slots), 0)
    misfit = jnp.zeros((tile_nodes, width), F32)
    for o in range(ny):
        onehot = (node_id == nodes[o, 0:1, 0:slots]).astype(F32).astype(BF)
        misfit = misfit + jnp.dot(
            onehot, received[o * slots : (o + 1) * slots], preferred_element_type=F32
        )
    grad[...] = scale[...] * misfit + prior[...]
    write(grad, grad_hbm)

    if done < rows - 2:
        interior(px, cw, rest, late, (rows - 2) // 2)
        write_part(rest, 1 + done, rows - 2 - done, 1, cols - 2)
    for part in (
        (0, 1, 0, cols),
        (rows - 1, 1, 0, cols),
        (1, rows - 2, 0, 1),
        (1, rows - 2, cols - 1, 1),
    ):
        product(px, cw, rest, *part)
        write_part(rest, *part)
    for copy in writes:
        copy.wait()


def kernel(
    nx, ny, early, late,
    x_hbm, c_hbm, lf_hbm, sc_hbm, live_hbm, tn_hbm,
    out_ref, px, cw, scale, prior, nodes_in, received,
    lf, sc, live, tn,
    face, face_stage, stage, x0, edge, halo0,
    lf_edge, lf_halo, lf_corner, field, once,
    nodes_out, pick, picked,
    local_sem, h0_send, h0_recv, hx_send, hx_recv, lf_send, lf_recv, lc_send, lc_recv,
    nd_send, nd_recv, pk_send, pk_recv,
):
    i, j = lax.axis_index("gx"), lax.axis_index("gy")
    rows, cols, layers, width = x_hbm.shape
    faces = rows * cols
    slots = faces // ny
    tile_a, tile_b = once.shape[0] - 2, cols
    tile_nodes = tile_a * tile_b
    low_a, high_a, low_b, high_b = i > 0, i < nx - 1, j > 0, j < ny - 1
    one = lambda flag: flag.astype(jnp.int32)
    up = lambda v, n: lax.rem(v + 1, n)
    down = lambda v, n: lax.rem(v + n - 1, n)
    to = [(down(i, nx), j), (up(i, nx), j), (i, down(j, ny)), (i, up(j, ny))]
    has_to = [low_a, high_a, low_b, high_b]
    has_from = [high_a, low_a, high_b, low_b]
    corner_to = [(to[a][0], to[2 + b][1]) for a in (0, 1) for b in (0, 1)]
    corner_has_to = [has_to[a] & has_to[2 + b] for a in (0, 1) for b in (0, 1)]
    corner_has_from = [has_from[a] & has_from[2 + b] for a in (0, 1) for b in (0, 1)]

    loads = [
        pltpu.make_async_copy(src, dst, local_sem.at[n])
        for n, (src, dst) in enumerate(
            [
                (x_hbm.at[0], face.at[0]),
                (x_hbm.at[rows - 1], face.at[1]),
                (x_hbm.at[:, 0], face.at[2]),
                (x_hbm.at[:, cols - 1], face.at[3]),
                (x_hbm, px.at[pl.ds(1, rows), pl.ds(1, cols)]),
                (lf_hbm, lf),
                (tn_hbm, tn),
                (live_hbm, live),
                (sc_hbm, sc),
                (c_hbm, cw),
            ]
        )
    ]

    barrier = pltpu.get_barrier_semaphore()
    for k in range(1, ny):
        pl.semaphore_signal(barrier, inc=1, device_id=(i, lax.rem(j + k, ny)), device_id_type=MESH)
    for flag, device in list(zip(has_to[:2], to[:2])) + list(zip(corner_has_to, corner_to)):

        @pl.when(flag)
        def _(device=device):
            pl.semaphore_signal(barrier, inc=1, device_id=device, device_id_type=MESH)

    partners = ny - 1 + (one(low_a) + one(high_a)) * (1 + one(low_b) + one(high_b))

    for load in loads:
        load.start()

    def zero_when(flag, ref, index):
        @pl.when(jnp.logical_not(flag))
        def _():
            ref[index] = jnp.zeros(ref.at[index].shape, ref.dtype)

    inner_a, inner_b = slice(1, rows + 1), slice(1, cols + 1)
    halo_at = [
        (rows + 1, inner_b),
        (0, inner_b),
        (inner_a, cols + 1),
        (inner_a, 0),
    ]
    for d in range(4):
        zero_when(has_from[d], px, halo_at[d])
        zero_when(has_from[d], halo0, d)
        zero_when(has_from[d], lf_halo, d)
        zero_when(corner_has_from[d], lf_corner, d)

    for d in range(4):
        loads[d].wait()
    face_stage[...] = face[...].astype(F32)[:, :, 0:8, :].reshape(face_stage.shape)
    for d in range(4):
        edge[d] = face_stage[pl.ds(8 * rows * d, rows, stride=8), :].astype(BF)

    def remote(src, dst, send, recv, device):
        return pltpu.make_async_remote_copy(
            src_ref=src, dst_ref=dst, send_sem=send, recv_sem=recv, device_id=device, device_id_type=MESH
        )

    layer_copies = [
        remote(edge.at[d], halo0.at[d], h0_send.at[d], h0_recv.at[d], to[d]) for d in range(4)
    ]
    x_edges = [x_hbm.at[0], x_hbm.at[rows - 1], x_hbm.at[:, 0], x_hbm.at[:, cols - 1]]
    x_halos = [
        px.at[rows + 1, pl.ds(1, cols)],
        px.at[0, pl.ds(1, cols)],
        px.at[pl.ds(1, rows), cols + 1],
        px.at[pl.ds(1, rows), 0],
    ]
    x_copies = [
        remote(x_edges[d], x_halos[d], hx_send.at[d], hx_recv.at[d], to[d]) for d in range(4)
    ]
    two = 2 * tile_b
    lf_srcs = [lf.at[pl.ds(0, two)], lf.at[pl.ds(tile_nodes - two, two)], lf_edge.at[0], lf_edge.at[1]]
    lf_dsts = [lf_halo.at[0], lf_halo.at[1], lf_halo.at[2, pl.ds(0, 2 * tile_a)], lf_halo.at[3, pl.ds(0, 2 * tile_a)]]
    lf_copies = [
        remote(lf_srcs[d], lf_dsts[d], lf_send.at[d], lf_recv.at[d], to[d]) for d in range(4)
    ]
    corner_rows = [0, tile_b - 8, tile_nodes - tile_b, tile_nodes - 8]
    corner_copies = [
        remote(lf.at[pl.ds(corner_rows[d], 8)], lf_corner.at[d], lc_send.at[d], lc_recv.at[d], corner_to[d])
        for d in range(4)
    ]

    def start_when(flag, copy):
        @pl.when(flag)
        def _():
            copy.start()

    pl.semaphore_wait(barrier, partners)
    for d in range(4):
        start_when(has_to[d], layer_copies[d])
    for d in range(4):
        start_when(has_to[d], x_copies[d])

    loads[5].wait()
    loads[6].wait()
    loads[7].wait()
    slot_id = lax.broadcasted_iota(jnp.int32, (1, slots), 1)
    nodes_out[...] = jnp.full(nodes_out.shape, -1, jnp.int32)
    for o in range(ny):
        count = live[0:1, o : o + 1]
        nodes_out[o, 0:1, 0:slots] = jnp.where(slot_id < count, tn[o : o + 1, :], -1)

    def row_copies(src, dst, send, recv, per_owner):
        sends, receives = [], []
        for k in range(1, ny):
            target, source = lax.rem(j + k, ny), lax.rem(j + ny - k, ny)
            sends.append(
                remote(src(target), dst(j), send.at[k - 1], recv.at[k - 1], (i, target))
            )
            receives.append(
                remote(src(target), dst(source), send.at[k - 1], recv.at[k - 1], (i, target))
            )
        return sends, receives

    node_sends, node_receives = row_copies(
        lambda o: nodes_out.at[o], lambda o: nodes_in.at[o], nd_send, nd_recv, 1
    )
    for copy in node_sends:
        copy.start()
    nodes_in[j] = nodes_out[j]

    lf_edge[0, 0:tile_a] = lf[pl.ds(0, tile_a, stride=tile_b), :]
    lf_edge[0, tile_a : 2 * tile_a] = lf[pl.ds(1, tile_a, stride=tile_b), :]
    lf_edge[1, 0:tile_a] = lf[pl.ds(tile_b - 2, tile_a, stride=tile_b), :]
    lf_edge[1, tile_a : 2 * tile_a] = lf[pl.ds(tile_b - 1, tile_a, stride=tile_b), :]
    for d in range(4):
        start_when(has_to[d], lf_copies[d])
    for d in range(4):
        start_when(corner_has_to[d], corner_copies[d])

    loads[4].wait()
    stage[...] = px[inner_a, inner_b].astype(F32)[:, :, 0:8, :].reshape(faces * 8, width)
    x0[inner_a, 8 : 8 + cols] = stage[pl.ds(0, faces, stride=8), :].reshape(rows, cols, width)

    loads[8].wait()
    column = jnp.broadcast_to(sc[0:1, :].astype(F32), (128, faces)).T
    for part in range(faces // 128):
        face_id = lax.broadcasted_iota(jnp.int32, (faces, 128), 1) + 128 * part
        pick[:, 128 * part : 128 * (part + 1)] = (column == face_id.astype(F32)).astype(BF)

    loads[9].wait()

    interior(px, cw, out_ref, 0, early)

    for d in range(4):
        pl.when(has_from[d])(layer_copies[d].wait_recv)
    x0[rows + 1, 8 : 8 + cols] = halo0[0].astype(F32)
    x0[0, 8 : 8 + cols] = halo0[1].astype(F32)
    x0[inner_a, 8 + cols : 9 + cols] = halo0[2].astype(F32).reshape(rows, 1, width)
    x0[inner_a, 7:8] = halo0[3].astype(F32).reshape(rows, 1, width)
    basal_terms = [
        x0[inner_a, 8 : 8 + cols].reshape(faces, width),
        stage[pl.ds(1, faces, stride=8), :],
        x0[0:rows, 8 : 8 + cols].reshape(faces, width),
        x0[2 : rows + 2, 8 : 8 + cols].reshape(faces, width),
        x0[inner_a, 7 : 7 + cols].reshape(faces, width),
        x0[inner_a, 9 : 9 + cols].reshape(faces, width),
    ]
    basal_lhs = jnp.concatenate([t.astype(BF) for t in basal_terms], axis=1)
    basal_w = jnp.concatenate([cw[0], cw[2:7].reshape(5 * width, width)], axis=0)
    basal = jnp.dot(basal_lhs, basal_w, preferred_element_type=F32).astype(BF)
    picked[...] = jnp.dot(pick[...], basal, preferred_element_type=F32).astype(BF)

    def slot_rows(ref):
        return lambda o: ref.at[pl.ds(pl.multiple_of(o * slots, slots), slots)]

    block_sends, block_receives = row_copies(
        slot_rows(picked), slot_rows(received), pk_send, pk_recv, slots
    )
    for copy in block_sends:
        copy.start()
    mine = pl.ds(pl.multiple_of(j * slots, slots), slots)
    received[mine, :] = picked[mine, :]

    interior(px, cw, out_ref, early, late)

    for d in range(4):
        pl.when(has_from[d])(lf_copies[d].wait_recv)
    for d in range(4):
        pl.when(corner_has_from[d])(corner_copies[d].wait_recv)
    field[...] = jnp.zeros_like(field)
    field[2 : 2 + tile_a, 8 : 8 + tile_b] = lf[...].reshape(tile_a, tile_b, width)
    field[2 + tile_a : 4 + tile_a, 8 : 8 + tile_b] = lf_halo[0].reshape(2, tile_b, width)
    field[0:2, 8 : 8 + tile_b] = lf_halo[1].reshape(2, tile_b, width)
    for side, at in ((2, 8 + tile_b), (3, 6)):
        for c in range(2):
            field[2 : 2 + tile_a, at + c : at + c + 1] = lf_halo[
                side, c * tile_a : (c + 1) * tile_a
            ].reshape(tile_a, 1, width)
    for d, (row, col, at) in enumerate(
        [(2 + tile_a, 8 + tile_b, 0), (2 + tile_a, 7, 7), (1, 8 + tile_b, 0), (1, 7, 7)]
    ):
        field[row, col : col + 1] = lf_corner[d, at : at + 1]

    def stencil(ref, a0, na, b0, nb):
        beside = (
            ref[a0 + 1 : a0 + 1 + na, b0 : b0 + nb]
            + ref[a0 - 1 : a0 - 1 + na, b0 : b0 + nb]
            + ref[a0 : a0 + na, b0 + 1 : b0 + 1 + nb]
            + ref[a0 : a0 + na, b0 - 1 : b0 - 1 + nb]
        )
        return 1.3 * ref[a0 : a0 + na, b0 : b0 + nb] - 0.2 * beside

    first = stencil(field, 1, tile_a + 2, 7, tile_b + 2)
    row_id = lax.broadcasted_iota(jnp.int32, first.shape, 0) + i * tile_a - 1
    col_id = lax.broadcasted_iota(jnp.int32, first.shape, 1) + j * tile_b - 1
    inside = (row_id >= 0) & (row_id < nx * tile_a) & (col_id >= 0) & (col_id < ny * tile_b)
    once[:, 7 : 9 + tile_b] = jnp.where(inside, first, 0.0)
    prior[...] = stencil(once, 1, tile_a, 8, tile_b).reshape(tile_nodes, width)
    scale[...] = jnp.exp(lf[...])

    for d in range(4):
        pl.when(has_from[d])(x_copies[d].wait_recv)
    for copy in node_receives + block_receives:
        copy.wait_recv()
    for d in range(4):
        pl.when(has_to[d])(layer_copies[d].wait_send)
        pl.when(has_to[d])(x_copies[d].wait_send)
        pl.when(has_to[d])(lf_copies[d].wait_send)
        pl.when(corner_has_to[d])(corner_copies[d].wait_send)
    for copy in node_sends + block_sends:
        copy.wait_send()


def solution(mesh):
    nx, ny = mesh.shape["gx"], mesh.shape["gy"]

    def per_device(adjoint_trace, coupling, log_friction, send_column, live_count, target_node):
        rows, cols, layers, width = adjoint_trace.shape
        tile_a, tile_b, _ = log_friction.shape
        tile_nodes = tile_a * tile_b
        faces = rows * cols
        slots = faces // ny
        vmem = pltpu.VMEM
        dma = pltpu.SemaphoreType.DMA
        hbm = pl.BlockSpec(memory_space=pltpu.HBM)
        local = pl.BlockSpec(memory_space=vmem)
        shape = jax.ShapeDtypeStruct
        early, late = 0, (rows - 2) // 2
        held = pl.pallas_call(
            functools.partial(kernel, nx, ny, early, late),
            out_shape=(
                shape(adjoint_trace.shape, BF),
                shape((rows + 2, cols + 2, layers, width), BF),
                shape(coupling.shape, BF),
                shape((tile_nodes, width), F32),
                shape((tile_nodes, width), F32),
                shape((ny, 8, 128), jnp.int32),
                shape((faces, width), BF),
            ),
            in_specs=[hbm] * 6,
            out_specs=(local,) * 7,
            scratch_shapes=[
                vmem((tile_nodes, width), F32),
                vmem((1, faces), jnp.int32),
                vmem((1, ny), jnp.int32),
                vmem((ny, slots), jnp.int32),
                vmem((4, rows, layers, width), BF),
                vmem((4 * rows * 8, width), F32),
                vmem((faces * 8, width), F32),
                vmem((rows + 2, cols + 16, width), F32),
                vmem((4, 16, width), BF),
                vmem((4, 16, width), BF),
                vmem((2, 2 * tile_a, width), F32),
                vmem((4, 2 * tile_b, width), F32),
                vmem((4, 8, width), F32),
                vmem((tile_a + 4, tile_b + 16, width), F32),
                vmem((tile_a + 2, tile_b + 16, width), F32),
                vmem((ny, 8, 128), jnp.int32),
                vmem((faces, faces), BF),
                vmem((faces, width), BF),
                dma((10,)),
                *[dma((4,)) for _ in range(8)],
                *[dma((ny - 1,)) for _ in range(4)],
            ],
            compiler_params=pltpu.CompilerParams(
                collective_id=0, has_side_effects=True, vmem_limit_bytes=24 * 2**20
            ),
            cost_estimate=pl.CostEstimate(
                flops=2 * 7 * faces * layers * width * width,
                bytes_accessed=4 * faces * layers * width,
                transcendentals=tile_nodes * width,
            ),
        )(
            *[
                pltpu.with_memory_space_constraint(operand, pltpu.HBM)
                for operand in (
                    adjoint_trace,
                    coupling,
                    log_friction.reshape(tile_nodes, width),
                    send_column.reshape(1, faces),
                    live_count.reshape(1, ny),
                    target_node.reshape(ny, slots),
                )
            ]
        )
        trace_update, gradient = pl.pallas_call(
            functools.partial(finish, ny, late),
            out_shape=(shape(adjoint_trace.shape, BF), shape((tile_nodes, width), F32)),
            in_specs=[local] * 7,
            out_specs=(hbm, hbm),
            scratch_shapes=[
                vmem(adjoint_trace.shape, BF),
                vmem((tile_nodes, width), F32),
                dma((8,)),
            ],
            compiler_params=pltpu.CompilerParams(vmem_limit_bytes=24 * 2**20),
        )(*held)
        return trace_update, gradient.reshape(tile_a, tile_b, width)

    in_specs = (
        P("gx", "gy", None, None),
        P(),
        P("gx", "gy", None),
        P("gx", "gy", None),
        P("gx", "gy", None),
        P("gx", "gy", None, None),
    )
    out_specs = (P("gx", "gy", None, None), P("gx", "gy", None))
    return jax.shard_map(
        per_device, mesh=mesh, in_specs=in_specs, out_specs=out_specs, check_vma=False
    )
```

```python
import functools

import jax
import jax.numpy as jnp
from jax import lax
from jax.experimental import pallas as pl
from jax.experimental.pallas import tpu as pltpu
from jax.sharding import PartitionSpec as P

MESH = pl.DeviceIdType.MESH
BF, F32 = jnp.bfloat16, jnp.float32


def product(px, cw, out_ref, a0, na, b0, nb):
    layers, width = px.shape[2:]
    own = px[pl.ds(a0 + 1, na), b0 + 1 : b0 + 1 + nb]
    count = na * nb
    wide = own.astype(F32).reshape(count, layers, width)
    layer = lax.broadcasted_iota(jnp.int32, wide.shape, 1)
    below = jnp.where(layer == 0, 0.0, pltpu.roll(wide, 1, 1)).astype(BF)
    above = jnp.where(layer == layers - 1, 0.0, pltpu.roll(wide, layers - 1, 1)).astype(BF)
    flat = lambda v: v.reshape(count * layers, width)
    terms = [
        own,
        below,
        above,
        px[pl.ds(a0, na), b0 + 1 : b0 + 1 + nb],
        px[pl.ds(a0 + 2, na), b0 + 1 : b0 + 1 + nb],
        px[pl.ds(a0 + 1, na), b0 : b0 + nb],
        px[pl.ds(a0 + 1, na), b0 + 2 : b0 + 2 + nb],
    ]
    lhs = jnp.concatenate([flat(t) for t in terms], axis=1)
    total = jnp.dot(lhs, cw[...].reshape(7 * width, width), preferred_element_type=F32)
    out_ref[pl.ds(a0, na), b0 : b0 + nb] = total.astype(BF).reshape(na, nb, layers, width)


def interior(px, cw, out_ref, first, count):
    product(px, cw, out_ref, first, count, 1, px.shape[1] - 4)


def finish(
    ny,
    inner, px, cw, scale, prior, nodes, received,
    out_hbm, grad_hbm,
    rest, grad, sem,
):
    rows, cols = inner.shape[:2]
    tile_nodes, width = scale.shape
    slots = received.shape[0] // ny
    writes = []

    def write(src, dst):
        copy = pltpu.make_async_copy(src, dst, sem.at[len(writes)])
        copy.start()
        writes.append(copy)

    def write_part(ref, a0, na, b0, nb):
        at = (pl.ds(a0, na), pl.ds(b0, nb))
        write(ref.at[at], out_hbm.at[at])

    write_part(inner, 1, rows - 2, 1, cols - 2)

    node_id = lax.broadcasted_iota(jnp.int32, (tile_nodes, slots), 0)
    misfit = jnp.zeros((tile_nodes, width), F32)
    for o in range(ny):
        onehot = (node_id == nodes[o, 0:1, 0:slots]).astype(F32).astype(BF)
        misfit = misfit + jnp.dot(
            onehot, received[o * slots : (o + 1) * slots], preferred_element_type=F32
        )
    grad[...] = scale[...] * misfit + prior[...]
    write(grad, grad_hbm)

    for part in (
        (0, 1, 0, cols),
        (rows - 1, 1, 0, cols),
        (1, rows - 2, 0, 1),
        (1, rows - 2, cols - 1, 1),
    ):
        product(px, cw, rest, *part)
        write_part(rest, *part)
    for copy in writes:
        copy.wait()


def kernel(
    nx, ny,
    x_hbm, c_hbm, lf_hbm, sc_hbm, live_hbm, tn_hbm,
    out_ref, px, cw, scale, prior, nodes_in, received,
    lf, sc, live, tn,
    face, face_stage, stage, x0, edge, halo0,
    lf_edge, lf_halo, lf_corner, field, once,
    nodes_out, pick, picked,
    local_sem, h0_send, h0_recv, hx_send, hx_recv, lf_send, lf_recv, lc_send, lc_recv,
    nd_send, nd_recv, pk_send, pk_recv,
):
    i, j = lax.axis_index("gx"), lax.axis_index("gy")
    rows, cols, layers, width = x_hbm.shape
    faces = rows * cols
    slots = faces // ny
    tile_a, tile_b = once.shape[0] - 2, cols
    tile_nodes = tile_a * tile_b
    low_a, high_a, low_b, high_b = i > 0, i < nx - 1, j > 0, j < ny - 1
    one = lambda flag: flag.astype(jnp.int32)
    up = lambda v, n: lax.rem(v + 1, n)
    down = lambda v, n: lax.rem(v + n - 1, n)
    to = [(down(i, nx), j), (up(i, nx), j), (i, down(j, ny)), (i, up(j, ny))]
    has_to = [low_a, high_a, low_b, high_b]
    has_from = [high_a, low_a, high_b, low_b]
    corner_to = [(to[a][0], to[2 + b][1]) for a in (0, 1) for b in (0, 1)]
    corner_has_to = [has_to[a] & has_to[2 + b] for a in (0, 1) for b in (0, 1)]
    corner_has_from = [has_from[a] & has_from[2 + b] for a in (0, 1) for b in (0, 1)]

    loads = [
        pltpu.make_async_copy(src, dst, local_sem.at[n])
        for n, (src, dst) in enumerate(
            [
                (x_hbm.at[0], face.at[0]),
                (x_hbm.at[rows - 1], face.at[1]),
                (x_hbm.at[:, 0], face.at[2]),
                (x_hbm.at[:, cols - 1], face.at[3]),
                (x_hbm, px.at[pl.ds(1, rows), pl.ds(1, cols)]),
                (lf_hbm, lf),
                (tn_hbm, tn),
                (live_hbm, live),
                (sc_hbm, sc),
                (c_hbm, cw),
            ]
        )
    ]

    barrier = pltpu.get_barrier_semaphore()
    for k in range(1, ny):
        pl.semaphore_signal(barrier, inc=1, device_id=(i, lax.rem(j + k, ny)), device_id_type=MESH)
    for flag, device in list(zip(has_to[:2], to[:2])) + list(zip(corner_has_to, corner_to)):

        @pl.when(flag)
        def _(device=device):
            pl.semaphore_signal(barrier, inc=1, device_id=device, device_id_type=MESH)

    partners = ny - 1 + (one(low_a) + one(high_a)) * (1 + one(low_b) + one(high_b))

    for load in loads:
        load.start()

    def zero_when(flag, ref, index):
        @pl.when(jnp.logical_not(flag))
        def _():
            ref[index] = jnp.zeros(ref.at[index].shape, ref.dtype)

    inner_a, inner_b = slice(1, rows + 1), slice(1, cols + 1)
    halo_at = [
        (rows + 1, inner_b),
        (0, inner_b),
        (inner_a, cols + 1),
        (inner_a, 0),
    ]
    for d in range(4):
        zero_when(has_from[d], px, halo_at[d])
    x0[...] = jnp.zeros_like(x0)
    field[...] = jnp.zeros_like(field)

    for d in range(4):
        loads[d].wait()
    face_stage[...] = face[...].astype(F32)[:, :, 0:8, :].reshape(face_stage.shape)
    for d in range(4):
        edge[d] = face_stage[pl.ds(8 * rows * d, rows, stride=8), :].astype(BF)

    def remote(src, dst, send, recv, device):
        return pltpu.make_async_remote_copy(
            src_ref=src, dst_ref=dst, send_sem=send, recv_sem=recv, device_id=device, device_id_type=MESH
        )

    layer_copies = [
        remote(edge.at[d], halo0.at[d], h0_send.at[d], h0_recv.at[d], to[d]) for d in range(4)
    ]
    x_edges = [x_hbm.at[0], x_hbm.at[rows - 1], x_hbm.at[:, 0], x_hbm.at[:, cols - 1]]
    x_halos = [
        px.at[rows + 1, pl.ds(1, cols)],
        px.at[0, pl.ds(1, cols)],
        px.at[pl.ds(1, rows), cols + 1],
        px.at[pl.ds(1, rows), 0],
    ]
    x_copies = [
        remote(x_edges[d], x_halos[d], hx_send.at[d], hx_recv.at[d], to[d]) for d in range(4)
    ]
    two = 2 * tile_b
    lf_srcs = [lf.at[pl.ds(0, two)], lf.at[pl.ds(tile_nodes - two, two)], lf_edge.at[0], lf_edge.at[1]]
    lf_dsts = [lf_halo.at[0], lf_halo.at[1], lf_halo.at[2, pl.ds(0, 2 * tile_a)], lf_halo.at[3, pl.ds(0, 2 * tile_a)]]
    lf_copies = [
        remote(lf_srcs[d], lf_dsts[d], lf_send.at[d], lf_recv.at[d], to[d]) for d in range(4)
    ]
    corner_rows = [0, tile_b - 8, tile_nodes - tile_b, tile_nodes - 8]
    corner_copies = [
        remote(lf.at[pl.ds(corner_rows[d], 8)], lf_corner.at[d], lc_send.at[d], lc_recv.at[d], corner_to[d])
        for d in range(4)
    ]

    def start_when(flag, copy):
        @pl.when(flag)
        def _():
            copy.start()

    pl.semaphore_wait(barrier, partners)
    for d in range(4):
        start_when(has_to[d], layer_copies[d])
    for d in range(4):
        start_when(has_to[d], x_copies[d])

    loads[5].wait()
    loads[6].wait()
    loads[7].wait()
    slot_id = lax.broadcasted_iota(jnp.int32, (1, slots), 1)
    nodes_out[...] = jnp.full(nodes_out.shape, -1, jnp.int32)
    for o in range(ny):
        count = live[0:1, o : o + 1]
        nodes_out[o, 0:1, 0:slots] = jnp.where(slot_id < count, tn[o : o + 1, :], -1)

    def row_copies(src, dst, send, recv, per_owner):
        sends, receives = [], []
        for k in range(1, ny):
            target, source = lax.rem(j + k, ny), lax.rem(j + ny - k, ny)
            sends.append(
                remote(src(target), dst(j), send.at[k - 1], recv.at[k - 1], (i, target))
            )
            receives.append(
                remote(src(target), dst(source), send.at[k - 1], recv.at[k - 1], (i, target))
            )
        return sends, receives

    node_sends, node_receives = row_copies(
        lambda o: nodes_out.at[o], lambda o: nodes_in.at[o], nd_send, nd_recv, 1
    )
    for copy in node_sends:
        copy.start()
    nodes_in[j] = nodes_out[j]

    lf_edge[0, 0:tile_a] = lf[pl.ds(0, tile_a, stride=tile_b), :]
    lf_edge[0, tile_a : 2 * tile_a] = lf[pl.ds(1, tile_a, stride=tile_b), :]
    lf_edge[1, 0:tile_a] = lf[pl.ds(tile_b - 2, tile_a, stride=tile_b), :]
    lf_edge[1, tile_a : 2 * tile_a] = lf[pl.ds(tile_b - 1, tile_a, stride=tile_b), :]
    for d in range(4):
        start_when(has_to[d], lf_copies[d])
    for d in range(4):
        start_when(corner_has_to[d], corner_copies[d])

    loads[4].wait()
    stage[...] = px[inner_a, inner_b].astype(F32)[:, :, 0:8, :].reshape(faces * 8, width)
    x0[inner_a, 8 : 8 + cols] = stage[pl.ds(0, faces, stride=8), :].reshape(rows, cols, width)

    loads[8].wait()
    column = jnp.broadcast_to(sc[0:1, :].astype(F32), (128, faces)).T
    for part in range(faces // 128):
        face_id = lax.broadcasted_iota(jnp.int32, (faces, 128), 1) + 128 * part
        pick[:, 128 * part : 128 * (part + 1)] = (column == face_id.astype(F32)).astype(BF)

    loads[9].wait()

    def basal_halo(d):
        layer_copies[d].wait_recv()
        block = halo0[d].astype(F32)
        if d < 2:
            x0[(rows + 1, 0)[d], 8 : 8 + cols] = block
        else:
            at = (8 + cols, 7)[d - 2]
            x0[inner_a, at : at + 1] = block.reshape(rows, 1, width)

    for d in range(4):
        pl.when(has_from[d])(functools.partial(basal_halo, d))
    basal_terms = [
        x0[inner_a, 8 : 8 + cols].reshape(faces, width),
        stage[pl.ds(1, faces, stride=8), :],
        x0[0:rows, 8 : 8 + cols].reshape(faces, width),
        x0[2 : rows + 2, 8 : 8 + cols].reshape(faces, width),
        x0[inner_a, 7 : 7 + cols].reshape(faces, width),
        x0[inner_a, 9 : 9 + cols].reshape(faces, width),
    ]
    basal_lhs = jnp.concatenate([t.astype(BF) for t in basal_terms], axis=1)
    basal_w = jnp.concatenate([cw[0], cw[2:7].reshape(5 * width, width)], axis=0)
    basal = jnp.dot(basal_lhs, basal_w, preferred_element_type=F32).astype(BF)
    picked[...] = jnp.dot(pick[...], basal, preferred_element_type=F32).astype(BF)

    def slot_rows(ref):
        return lambda o: ref.at[pl.ds(pl.multiple_of(o * slots, slots), slots)]

    block_sends, block_receives = row_copies(
        slot_rows(picked), slot_rows(received), pk_send, pk_recv, slots
    )
    for copy in block_sends:
        copy.start()
    mine = pl.ds(pl.multiple_of(j * slots, slots), slots)
    received[mine, :] = picked[mine, :]

    half = (rows - 2) // 2
    interior(px, cw, out_ref, 1, half)
    interior(px, cw, out_ref, 1 + half, rows - 2 - half)

    field[2 : 2 + tile_a, 8 : 8 + tile_b] = lf[...].reshape(tile_a, tile_b, width)

    def field_halo(d):
        lf_copies[d].wait_recv()
        if d < 2:
            at = (2 + tile_a, 0)[d]
            field[at : at + 2, 8 : 8 + tile_b] = lf_halo[d].reshape(2, tile_b, width)
        else:
            at = (8 + tile_b, 6)[d - 2]
            for c in range(2):
                field[2 : 2 + tile_a, at + c : at + c + 1] = lf_halo[
                    d, c * tile_a : (c + 1) * tile_a
                ].reshape(tile_a, 1, width)

    def field_corner(d):
        corner_copies[d].wait_recv()
        row, at = (2 + tile_a, 1)[d // 2], (8 + tile_b, 7)[d % 2]
        source = (0, 7)[d % 2]
        field[row, at : at + 1] = lf_corner[d, source : source + 1]

    for d in range(4):
        pl.when(has_from[d])(functools.partial(field_halo, d))
    for d in range(4):
        pl.when(corner_has_from[d])(functools.partial(field_corner, d))

    def stencil(ref, a0, na, b0, nb):
        beside = (
            ref[a0 + 1 : a0 + 1 + na, b0 : b0 + nb]
            + ref[a0 - 1 : a0 - 1 + na, b0 : b0 + nb]
            + ref[a0 : a0 + na, b0 + 1 : b0 + 1 + nb]
            + ref[a0 : a0 + na, b0 - 1 : b0 - 1 + nb]
        )
        return 1.3 * ref[a0 : a0 + na, b0 : b0 + nb] - 0.2 * beside

    first = stencil(field, 1, tile_a + 2, 7, tile_b + 2)
    row_id = lax.broadcasted_iota(jnp.int32, first.shape, 0) + i * tile_a - 1
    col_id = lax.broadcasted_iota(jnp.int32, first.shape, 1) + j * tile_b - 1
    inside = (row_id >= 0) & (row_id < nx * tile_a) & (col_id >= 0) & (col_id < ny * tile_b)
    once[:, 7 : 9 + tile_b] = jnp.where(inside, first, 0.0)
    prior[...] = stencil(once, 1, tile_a, 8, tile_b).reshape(tile_nodes, width)
    scale[...] = jnp.exp(lf[...])

    for d in range(4):
        pl.when(has_from[d])(x_copies[d].wait_recv)
    for copy in node_receives + block_receives:
        copy.wait_recv()
    def sent(d):
        layer_copies[d].wait_send()
        x_copies[d].wait_send()
        lf_copies[d].wait_send()

    for d in range(4):
        pl.when(has_to[d])(functools.partial(sent, d))
        pl.when(corner_has_to[d])(corner_copies[d].wait_send)
    for copy in node_sends + block_sends:
        copy.wait_send()


def solution(mesh):
    nx, ny = mesh.shape["gx"], mesh.shape["gy"]

    def per_device(adjoint_trace, coupling, log_friction, send_column, live_count, target_node):
        rows, cols, layers, width = adjoint_trace.shape
        tile_a, tile_b, _ = log_friction.shape
        tile_nodes = tile_a * tile_b
        faces = rows * cols
        slots = faces // ny
        vmem = pltpu.VMEM
        dma = pltpu.SemaphoreType.DMA
        hbm = pl.BlockSpec(memory_space=pltpu.HBM)
        local = pl.BlockSpec(memory_space=vmem)
        shape = jax.ShapeDtypeStruct
        held = pl.pallas_call(
            functools.partial(kernel, nx, ny),
            out_shape=(
                shape(adjoint_trace.shape, BF),
                shape((rows + 2, cols + 2, layers, width), BF),
                shape(coupling.shape, BF),
                shape((tile_nodes, width), F32),
                shape((tile_nodes, width), F32),
                shape((ny, 8, 128), jnp.int32),
                shape((faces, width), BF),
            ),
            in_specs=[hbm] * 6,
            out_specs=(local,) * 7,
            scratch_shapes=[
                vmem((tile_nodes, width), F32),
                vmem((1, faces), jnp.int32),
                vmem((1, ny), jnp.int32),
                vmem((ny, slots), jnp.int32),
                vmem((4, rows, layers, width), BF),
                vmem((4 * rows * 8, width), F32),
                vmem((faces * 8, width), F32),
                vmem((rows + 2, cols + 16, width), F32),
                vmem((4, 16, width), BF),
                vmem((4, 16, width), BF),
                vmem((2, 2 * tile_a, width), F32),
                vmem((4, 2 * tile_b, width), F32),
                vmem((4, 8, width), F32),
                vmem((tile_a + 4, tile_b + 16, width), F32),
                vmem((tile_a + 2, tile_b + 16, width), F32),
                vmem((ny, 8, 128), jnp.int32),
                vmem((faces, faces), BF),
                vmem((faces, width), BF),
                dma((10,)),
                *[dma((4,)) for _ in range(8)],
                *[dma((ny - 1,)) for _ in range(4)],
            ],
            compiler_params=pltpu.CompilerParams(
                collective_id=0, has_side_effects=True, vmem_limit_bytes=24 * 2**20
            ),
            cost_estimate=pl.CostEstimate(
                flops=2 * 7 * faces * layers * width * width,
                bytes_accessed=4 * faces * layers * width,
                transcendentals=tile_nodes * width,
            ),
        )(
            *[
                pltpu.with_memory_space_constraint(operand, pltpu.HBM)
                for operand in (
                    adjoint_trace,
                    coupling,
                    log_friction.reshape(tile_nodes, width),
                    send_column.reshape(1, faces),
                    live_count.reshape(1, ny),
                    target_node.reshape(ny, slots),
                )
            ]
        )
        trace_update, gradient = pl.pallas_call(
            functools.partial(finish, ny),
            out_shape=(shape(adjoint_trace.shape, BF), shape((tile_nodes, width), F32)),
            in_specs=[local] * 7,
            out_specs=(hbm, hbm),
            scratch_shapes=[
                vmem(adjoint_trace.shape, BF),
                vmem((tile_nodes, width), F32),
                dma((8,)),
            ],
            compiler_params=pltpu.CompilerParams(vmem_limit_bytes=24 * 2**20),
        )(*held)
        return trace_update, gradient.reshape(tile_a, tile_b, width)

    in_specs = (
        P("gx", "gy", None, None),
        P(),
        P("gx", "gy", None),
        P("gx", "gy", None),
        P("gx", "gy", None),
        P("gx", "gy", None, None),
    )
    out_specs = (P("gx", "gy", None, None), P("gx", "gy", None))
    return jax.shard_map(
        per_device, mesh=mesh, in_specs=in_specs, out_specs=out_specs, check_vma=False
    )
```

```python
import functools

import jax
import jax.numpy as jnp
from jax import lax
from jax.experimental import pallas as pl
from jax.experimental.pallas import tpu as pltpu
from jax.sharding import PartitionSpec as P

MESH = pl.DeviceIdType.MESH
BF, F32 = jnp.bfloat16, jnp.float32


def product(px, cw, out_ref, a0, na, b0, nb):
    layers, width = px.shape[2:]
    own = px[pl.ds(a0 + 1, na), b0 + 1 : b0 + 1 + nb]
    count = na * nb
    wide = own.astype(F32).reshape(count, layers, width)
    layer = lax.broadcasted_iota(jnp.int32, wide.shape, 1)
    below = jnp.where(layer == 0, 0.0, pltpu.roll(wide, 1, 1)).astype(BF)
    above = jnp.where(layer == layers - 1, 0.0, pltpu.roll(wide, layers - 1, 1)).astype(BF)
    flat = lambda v: v.reshape(count * layers, width)
    terms = [
        own,
        below,
        above,
        px[pl.ds(a0, na), b0 + 1 : b0 + 1 + nb],
        px[pl.ds(a0 + 2, na), b0 + 1 : b0 + 1 + nb],
        px[pl.ds(a0 + 1, na), b0 : b0 + nb],
        px[pl.ds(a0 + 1, na), b0 + 2 : b0 + 2 + nb],
    ]
    lhs = jnp.concatenate([flat(t) for t in terms], axis=1)
    total = jnp.dot(lhs, cw[...].reshape(7 * width, width), preferred_element_type=F32)
    out_ref[pl.ds(a0, na), b0 : b0 + nb] = total.astype(BF).reshape(na, nb, layers, width)


def interior(px, cw, out_ref, first, count):
    product(px, cw, out_ref, first, count, 1, px.shape[1] - 4)


def finish(
    ny,
    inner, px, cw, scale, prior, nodes, received,
    out_hbm, grad_hbm,
    rest, grad, sem,
):
    rows, cols = inner.shape[:2]
    tile_nodes, width = scale.shape
    slots = received.shape[0] // ny
    writes = []

    def write(src, dst):
        copy = pltpu.make_async_copy(src, dst, sem.at[len(writes)])
        copy.start()
        writes.append(copy)

    def write_part(ref, a0, na, b0, nb):
        at = (pl.ds(a0, na), pl.ds(b0, nb))
        write(ref.at[at], out_hbm.at[at])

    write_part(inner, 1, rows - 2, 1, cols - 2)

    node_id = lax.broadcasted_iota(jnp.int32, (tile_nodes, slots), 0)
    misfit = jnp.zeros((tile_nodes, width), F32)
    for o in range(ny):
        onehot = (node_id == nodes[o, 0:1, 0:slots]).astype(F32).astype(BF)
        misfit = misfit + jnp.dot(
            onehot, received[o * slots : (o + 1) * slots], preferred_element_type=F32
        )
    grad[...] = scale[...] * misfit + prior[...]
    write(grad, grad_hbm)

    for part in (
        (0, 1, 0, cols),
        (rows - 1, 1, 0, cols),
        (1, rows - 2, 0, 1),
        (1, rows - 2, cols - 1, 1),
    ):
        product(px, cw, rest, *part)
        write_part(rest, *part)
    for copy in writes:
        copy.wait()


def kernel(
    nx, ny,
    x_hbm, c_hbm, lf_hbm, sc_hbm, live_hbm, tn_hbm,
    out_ref, px, cw, scale, prior, nodes_in, received,
    lf, sc, live, tn,
    face, face_stage, stage, x0, edge, halo0,
    lf_stage, lf_edge, lf_halo, lf_corner, field, once,
    nodes_out, pick, picked,
    local_sem, h0_send, h0_recv, hx_send, hx_recv, lf_send, lf_recv, lc_send, lc_recv,
    nd_send, nd_recv, pk_send, pk_recv,
):
    i, j = lax.axis_index("gx"), lax.axis_index("gy")
    rows, cols, layers, width = x_hbm.shape
    faces = rows * cols
    slots = faces // ny
    tile_a, tile_b = once.shape[0] - 2, cols
    tile_nodes = tile_a * tile_b
    low_a, high_a, low_b, high_b = i > 0, i < nx - 1, j > 0, j < ny - 1
    one = lambda flag: flag.astype(jnp.int32)
    up = lambda v, n: lax.rem(v + 1, n)
    down = lambda v, n: lax.rem(v + n - 1, n)
    to = [(down(i, nx), j), (up(i, nx), j), (i, down(j, ny)), (i, up(j, ny))]
    has_to = [low_a, high_a, low_b, high_b]
    has_from = [high_a, low_a, high_b, low_b]
    corner_to = [(to[a][0], to[2 + b][1]) for a in (0, 1) for b in (0, 1)]
    corner_has_to = [has_to[a] & has_to[2 + b] for a in (0, 1) for b in (0, 1)]
    corner_has_from = [has_from[a] & has_from[2 + b] for a in (0, 1) for b in (0, 1)]

    loads = [
        pltpu.make_async_copy(src, dst, local_sem.at[n])
        for n, (src, dst) in enumerate(
            [
                (x_hbm.at[0], face.at[0]),
                (x_hbm.at[rows - 1], face.at[1]),
                (x_hbm.at[:, 0], face.at[2]),
                (x_hbm.at[:, cols - 1], face.at[3]),
                (x_hbm, px.at[pl.ds(1, rows), pl.ds(1, cols)]),
                (lf_hbm, lf),
                (tn_hbm, tn),
                (live_hbm, live),
                (sc_hbm, sc),
                (c_hbm, cw),
            ]
        )
    ]

    barrier = pltpu.get_barrier_semaphore()
    for k in range(1, ny):
        pl.semaphore_signal(barrier, inc=1, device_id=(i, lax.rem(j + k, ny)), device_id_type=MESH)
    for flag, device in list(zip(has_to[:2], to[:2])) + list(zip(corner_has_to, corner_to)):

        @pl.when(flag)
        def _(device=device):
            pl.semaphore_signal(barrier, inc=1, device_id=device, device_id_type=MESH)

    partners = ny - 1 + (one(low_a) + one(high_a)) * (1 + one(low_b) + one(high_b))

    for load in loads:
        load.start()

    def zero_when(flag, ref, index):
        @pl.when(jnp.logical_not(flag))
        def _():
            ref[index] = jnp.zeros(ref.at[index].shape, ref.dtype)

    inner_a, inner_b = slice(1, rows + 1), slice(1, cols + 1)
    halo_at = [
        (rows + 1, inner_b),
        (0, inner_b),
        (inner_a, cols + 1),
        (inner_a, 0),
    ]
    for d in range(4):
        zero_when(has_from[d], px, halo_at[d])
    x0[...] = jnp.zeros_like(x0)
    field[...] = jnp.zeros_like(field)

    for d in range(4):
        loads[d].wait()
    face_stage[...] = face[...].astype(F32)[:, :, 0:8, :].reshape(face_stage.shape)
    for d in range(4):
        edge[d] = face_stage[pl.ds(8 * rows * d, rows, stride=8), :].astype(BF)

    def remote(src, dst, send, recv, device):
        return pltpu.make_async_remote_copy(
            src_ref=src, dst_ref=dst, send_sem=send, recv_sem=recv, device_id=device, device_id_type=MESH
        )

    layer_copies = [
        remote(edge.at[d], halo0.at[d], h0_send.at[d], h0_recv.at[d], to[d]) for d in range(4)
    ]
    x_edges = [x_hbm.at[0], x_hbm.at[rows - 1], x_hbm.at[:, 0], x_hbm.at[:, cols - 1]]
    x_halos = [
        px.at[rows + 1, pl.ds(1, cols)],
        px.at[0, pl.ds(1, cols)],
        px.at[pl.ds(1, rows), cols + 1],
        px.at[pl.ds(1, rows), 0],
    ]
    x_copies = [
        remote(x_edges[d], x_halos[d], hx_send.at[d], hx_recv.at[d], to[d]) for d in range(4)
    ]
    two = 2 * tile_b
    lf_srcs = [lf_edge.at[0], lf_edge.at[1], lf_edge.at[2, pl.ds(0, 2 * tile_a)], lf_edge.at[3, pl.ds(0, 2 * tile_a)]]
    lf_dsts = [lf_halo.at[0], lf_halo.at[1], lf_halo.at[2, pl.ds(0, 2 * tile_a)], lf_halo.at[3, pl.ds(0, 2 * tile_a)]]
    lf_copies = [
        remote(lf_srcs[d], lf_dsts[d], lf_send.at[d], lf_recv.at[d], to[d]) for d in range(4)
    ]
    corner_rows = [0, tile_b - 8, tile_nodes - tile_b, tile_nodes - 8]
    corner_copies = [
        remote(lf.at[pl.ds(corner_rows[d], 8)], lf_corner.at[d], lc_send.at[d], lc_recv.at[d], corner_to[d])
        for d in range(4)
    ]

    def start_when(flag, copy):
        @pl.when(flag)
        def _():
            copy.start()

    pl.semaphore_wait(barrier, partners)
    for d in range(4):
        start_when(has_to[d], layer_copies[d])
    for d in range(2):
        start_when(has_to[d], x_copies[d])

    loads[5].wait()
    loads[6].wait()
    loads[7].wait()
    slot_id = lax.broadcasted_iota(jnp.int32, (1, slots), 1)
    nodes_out[...] = jnp.full(nodes_out.shape, -1, jnp.int32)
    for o in range(ny):
        count = live[0:1, o : o + 1]
        nodes_out[o, 0:1, 0:slots] = jnp.where(slot_id < count, tn[o : o + 1, :], -1)

    def row_copies(src, dst, send, recv, per_owner):
        sends, receives = [], []
        for k in range(1, ny):
            target, source = lax.rem(j + k, ny), lax.rem(j + ny - k, ny)
            sends.append(
                remote(src(target), dst(j), send.at[k - 1], recv.at[k - 1], (i, target))
            )
            receives.append(
                remote(src(target), dst(source), send.at[k - 1], recv.at[k - 1], (i, target))
            )
        return sends, receives

    node_sends, node_receives = row_copies(
        lambda o: nodes_out.at[o], lambda o: nodes_in.at[o], nd_send, nd_recv, 1
    )
    nodes_in[j] = nodes_out[j]

    lf_edge[0] = lf[0:two].astype(BF)
    lf_edge[1] = lf[tile_nodes - two : tile_nodes].astype(BF)
    for d, first in ((2, 0), (3, tile_b - 2)):
        for c in range(2):
            lf_stage[c * tile_a : (c + 1) * tile_a] = lf[pl.ds(first + c, tile_a, stride=tile_b), :]
        lf_edge[d, 0 : 2 * tile_a] = lf_stage[...].astype(BF)

    loads[4].wait()
    stage[...] = px[inner_a, inner_b].astype(F32)[:, :, 0:8, :].reshape(faces * 8, width)
    x0[inner_a, 8 : 8 + cols] = stage[pl.ds(0, faces, stride=8), :].reshape(rows, cols, width)

    loads[8].wait()
    column = jnp.broadcast_to(sc[0:1, :].astype(F32), (128, faces)).T
    for part in range(faces // 128):
        face_id = lax.broadcasted_iota(jnp.int32, (faces, 128), 1) + 128 * part
        pick[:, 128 * part : 128 * (part + 1)] = (column == face_id.astype(F32)).astype(BF)

    loads[9].wait()

    def basal_halo(d):
        layer_copies[d].wait_recv()
        block = halo0[d].astype(F32)
        if d < 2:
            x0[(rows + 1, 0)[d], 8 : 8 + cols] = block
        else:
            at = (8 + cols, 7)[d - 2]
            x0[inner_a, at : at + 1] = block.reshape(rows, 1, width)

    for d in range(4):
        pl.when(has_from[d])(functools.partial(basal_halo, d))
    basal_terms = [
        x0[inner_a, 8 : 8 + cols].reshape(faces, width),
        stage[pl.ds(1, faces, stride=8), :],
        x0[0:rows, 8 : 8 + cols].reshape(faces, width),
        x0[2 : rows + 2, 8 : 8 + cols].reshape(faces, width),
        x0[inner_a, 7 : 7 + cols].reshape(faces, width),
        x0[inner_a, 9 : 9 + cols].reshape(faces, width),
    ]
    basal_lhs = jnp.concatenate([t.astype(BF) for t in basal_terms], axis=1)
    basal_w = jnp.concatenate([cw[0], cw[2:7].reshape(5 * width, width)], axis=0)
    basal = jnp.dot(basal_lhs, basal_w, preferred_element_type=F32).astype(BF)
    picked[...] = jnp.dot(pick[...], basal, preferred_element_type=F32).astype(BF)

    def slot_rows(ref):
        return lambda o: ref.at[pl.ds(pl.multiple_of(o * slots, slots), slots)]

    block_sends, block_receives = row_copies(
        slot_rows(picked), slot_rows(received), pk_send, pk_recv, slots
    )
    for copy in block_sends:
        copy.start()
    for copy in node_sends:
        copy.start()
    for d in range(4):
        start_when(has_to[d], lf_copies[d])
    for d in range(4):
        start_when(corner_has_to[d], corner_copies[d])
    for d in range(2, 4):
        start_when(has_to[d], x_copies[d])
    mine = pl.ds(pl.multiple_of(j * slots, slots), slots)
    received[mine, :] = picked[mine, :]

    half = (rows - 2) // 2
    interior(px, cw, out_ref, 1, half)
    interior(px, cw, out_ref, 1 + half, rows - 2 - half)

    field[2 : 2 + tile_a, 8 : 8 + tile_b] = lf[...].reshape(tile_a, tile_b, width)

    def field_halo(d):
        lf_copies[d].wait_recv()
        if d < 2:
            at = (2 + tile_a, 0)[d]
            field[at : at + 2, 8 : 8 + tile_b] = lf_halo[d].astype(F32).reshape(2, tile_b, width)
        else:
            at = (8 + tile_b, 6)[d - 2]
            block = lf_halo[d, 0 : 2 * tile_a].astype(F32)
            for c in range(2):
                field[2 : 2 + tile_a, at + c : at + c + 1] = block[
                    c * tile_a : (c + 1) * tile_a
                ].reshape(tile_a, 1, width)

    def field_corner(d):
        corner_copies[d].wait_recv()
        row, at = (2 + tile_a, 1)[d // 2], (8 + tile_b, 7)[d % 2]
        source = (0, 7)[d % 2]
        field[row, at : at + 1] = lf_corner[d, source : source + 1]

    for d in range(4):
        pl.when(has_from[d])(functools.partial(field_halo, d))
    for d in range(4):
        pl.when(corner_has_from[d])(functools.partial(field_corner, d))

    def stencil(ref, a0, na, b0, nb):
        beside = (
            ref[a0 + 1 : a0 + 1 + na, b0 : b0 + nb]
            + ref[a0 - 1 : a0 - 1 + na, b0 : b0 + nb]
            + ref[a0 : a0 + na, b0 + 1 : b0 + 1 + nb]
            + ref[a0 : a0 + na, b0 - 1 : b0 - 1 + nb]
        )
        return 1.3 * ref[a0 : a0 + na, b0 : b0 + nb] - 0.2 * beside

    first = stencil(field, 1, tile_a + 2, 7, tile_b + 2)
    row_id = lax.broadcasted_iota(jnp.int32, first.shape, 0) + i * tile_a - 1
    col_id = lax.broadcasted_iota(jnp.int32, first.shape, 1) + j * tile_b - 1
    inside = (row_id >= 0) & (row_id < nx * tile_a) & (col_id >= 0) & (col_id < ny * tile_b)
    once[:, 7 : 9 + tile_b] = jnp.where(inside, first, 0.0)
    prior[...] = stencil(once, 1, tile_a, 8, tile_b).reshape(tile_nodes, width)
    scale[...] = jnp.exp(lf[...])

    for d in range(4):
        pl.when(has_from[d])(x_copies[d].wait_recv)
    for copy in node_receives + block_receives:
        copy.wait_recv()
    def sent(d):
        layer_copies[d].wait_send()
        x_copies[d].wait_send()
        lf_copies[d].wait_send()

    for d in range(4):
        pl.when(has_to[d])(functools.partial(sent, d))
        pl.when(corner_has_to[d])(corner_copies[d].wait_send)
    for copy in node_sends + block_sends:
        copy.wait_send()


def solution(mesh):
    nx, ny = mesh.shape["gx"], mesh.shape["gy"]

    def per_device(adjoint_trace, coupling, log_friction, send_column, live_count, target_node):
        rows, cols, layers, width = adjoint_trace.shape
        tile_a, tile_b, _ = log_friction.shape
        tile_nodes = tile_a * tile_b
        faces = rows * cols
        slots = faces // ny
        vmem = pltpu.VMEM
        dma = pltpu.SemaphoreType.DMA
        hbm = pl.BlockSpec(memory_space=pltpu.HBM)
        local = pl.BlockSpec(memory_space=vmem)
        shape = jax.ShapeDtypeStruct
        held = pl.pallas_call(
            functools.partial(kernel, nx, ny),
            out_shape=(
                shape(adjoint_trace.shape, BF),
                shape((rows + 2, cols + 2, layers, width), BF),
                shape(coupling.shape, BF),
                shape((tile_nodes, width), F32),
                shape((tile_nodes, width), F32),
                shape((ny, 8, 128), jnp.int32),
                shape((faces, width), BF),
            ),
            in_specs=[hbm] * 6,
            out_specs=(local,) * 7,
            scratch_shapes=[
                vmem((tile_nodes, width), F32),
                vmem((1, faces), jnp.int32),
                vmem((1, ny), jnp.int32),
                vmem((ny, slots), jnp.int32),
                vmem((4, rows, layers, width), BF),
                vmem((4 * rows * 8, width), F32),
                vmem((faces * 8, width), F32),
                vmem((rows + 2, cols + 16, width), F32),
                vmem((4, 16, width), BF),
                vmem((4, 16, width), BF),
                vmem((2 * tile_a, width), F32),
                vmem((4, 2 * tile_b, width), BF),
                vmem((4, 2 * tile_b, width), BF),
                vmem((4, 8, width), F32),
                vmem((tile_a + 4, tile_b + 16, width), F32),
                vmem((tile_a + 2, tile_b + 16, width), F32),
                vmem((ny, 8, 128), jnp.int32),
                vmem((faces, faces), BF),
                vmem((faces, width), BF),
                dma((10,)),
                *[dma((4,)) for _ in range(8)],
                *[dma((ny - 1,)) for _ in range(4)],
            ],
            compiler_params=pltpu.CompilerParams(
                collective_id=0, has_side_effects=True, vmem_limit_bytes=24 * 2**20
            ),
            cost_estimate=pl.CostEstimate(
                flops=2 * 7 * faces * layers * width * width,
                bytes_accessed=4 * faces * layers * width,
                transcendentals=tile_nodes * width,
            ),
        )(
            *[
                pltpu.with_memory_space_constraint(operand, pltpu.HBM)
                for operand in (
                    adjoint_trace,
                    coupling,
                    log_friction.reshape(tile_nodes, width),
                    send_column.reshape(1, faces),
                    live_count.reshape(1, ny),
                    target_node.reshape(ny, slots),
                )
            ]
        )
        trace_update, gradient = pl.pallas_call(
            functools.partial(finish, ny),
            out_shape=(shape(adjoint_trace.shape, BF), shape((tile_nodes, width), F32)),
            in_specs=[local] * 7,
            out_specs=(hbm, hbm),
            scratch_shapes=[
                vmem(adjoint_trace.shape, BF),
                vmem((tile_nodes, width), F32),
                dma((8,)),
            ],
            compiler_params=pltpu.CompilerParams(vmem_limit_bytes=24 * 2**20),
        )(*held)
        return trace_update, gradient.reshape(tile_a, tile_b, width)

    in_specs = (
        P("gx", "gy", None, None),
        P(),
        P("gx", "gy", None),
        P("gx", "gy", None),
        P("gx", "gy", None),
        P("gx", "gy", None, None),
    )
    out_specs = (P("gx", "gy", None, None), P("gx", "gy", None))
    return jax.shard_map(
        per_device, mesh=mesh, in_specs=in_specs, out_specs=out_specs, check_vma=False
    )
```

```python
import functools

import jax
import jax.numpy as jnp
from jax import lax
from jax.experimental import pallas as pl
from jax.experimental.pallas import tpu as pltpu
from jax.sharding import PartitionSpec as P

MESH = pl.DeviceIdType.MESH
BF, F32 = jnp.bfloat16, jnp.float32


def product(px, cw, out_ref, a0, na, b0, nb):
    layers, width = px.shape[2:]
    own = px[pl.ds(a0 + 1, na), b0 + 1 : b0 + 1 + nb]
    count = na * nb
    wide = own.astype(F32).reshape(count, layers, width)
    layer = lax.broadcasted_iota(jnp.int32, wide.shape, 1)
    below = jnp.where(layer == 0, 0.0, pltpu.roll(wide, 1, 1)).astype(BF)
    above = jnp.where(layer == layers - 1, 0.0, pltpu.roll(wide, layers - 1, 1)).astype(BF)
    flat = lambda v: v.reshape(count * layers, width)
    terms = [
        own,
        below,
        above,
        px[pl.ds(a0, na), b0 + 1 : b0 + 1 + nb],
        px[pl.ds(a0 + 2, na), b0 + 1 : b0 + 1 + nb],
        px[pl.ds(a0 + 1, na), b0 : b0 + nb],
        px[pl.ds(a0 + 1, na), b0 + 2 : b0 + 2 + nb],
    ]
    lhs = jnp.concatenate([flat(t) for t in terms], axis=1)
    total = jnp.dot(lhs, cw[...].reshape(7 * width, width), preferred_element_type=F32)
    out_ref[pl.ds(a0, na), b0 : b0 + nb] = total.astype(BF).reshape(na, nb, layers, width)


def interior(px, cw, out_ref, first, count):
    product(px, cw, out_ref, first, count, 1, px.shape[1] - 4)


def finish(
    ny,
    inner, px, cw, scale, prior, nodes, received,
    out_hbm, grad_hbm,
    rest, grad, sem,
):
    rows, cols = inner.shape[:2]
    tile_nodes, width = scale.shape
    slots = received.shape[0] // ny
    writes = []

    def write(src, dst):
        copy = pltpu.make_async_copy(src, dst, sem.at[len(writes)])
        copy.start()
        writes.append(copy)

    def write_part(ref, a0, na, b0, nb):
        at = (pl.ds(a0, na), pl.ds(b0, nb))
        write(ref.at[at], out_hbm.at[at])

    write_part(inner, 1, rows - 2, 1, cols - 2)

    node_id = lax.broadcasted_iota(jnp.int32, (tile_nodes, slots), 0)
    misfit = jnp.zeros((tile_nodes, width), F32)
    for o in range(ny):
        onehot = (node_id == nodes[o, 0:1, 0:slots]).astype(F32).astype(BF)
        misfit = misfit + jnp.dot(
            onehot, received[o * slots : (o + 1) * slots], preferred_element_type=F32
        )
    grad[...] = scale[...] * misfit + prior[...]
    write(grad, grad_hbm)

    for part in (
        (0, 1, 0, cols),
        (rows - 1, 1, 0, cols),
        (1, rows - 2, 0, 1),
        (1, rows - 2, cols - 1, 1),
    ):
        product(px, cw, rest, *part)
        write_part(rest, *part)
    for copy in writes:
        copy.wait()


def kernel(
    nx, ny,
    x_hbm, c_hbm, lf_hbm, sc_hbm, live_hbm, tn_hbm,
    out_ref, px, cw, scale, prior, nodes_in, received,
    lf, sc, live, tn,
    face, face_stage, stage, x0, edge, halo0,
    lf_stage, lf_edge, lf_halo, lf_corner, field, once,
    nodes_out, pick, picked,
    local_sem, h0_send, h0_recv, hx_send, hx_recv, lf_send, lf_recv, lc_send, lc_recv,
    nd_send, nd_recv, pk_send, pk_recv,
):
    i, j = lax.axis_index("gx"), lax.axis_index("gy")
    rows, cols, layers, width = x_hbm.shape
    faces = rows * cols
    slots = faces // ny
    tile_a, tile_b = once.shape[0] - 2, cols
    tile_nodes = tile_a * tile_b
    low_a, high_a, low_b, high_b = i > 0, i < nx - 1, j > 0, j < ny - 1
    one = lambda flag: flag.astype(jnp.int32)
    up = lambda v, n: lax.rem(v + 1, n)
    down = lambda v, n: lax.rem(v + n - 1, n)
    to = [(down(i, nx), j), (up(i, nx), j), (i, down(j, ny)), (i, up(j, ny))]
    has_to = [low_a, high_a, low_b, high_b]
    has_from = [high_a, low_a, high_b, low_b]
    corner_to = [(to[a][0], to[2 + b][1]) for a in (0, 1) for b in (0, 1)]
    corner_has_to = [has_to[a] & has_to[2 + b] for a in (0, 1) for b in (0, 1)]
    corner_has_from = [has_from[a] & has_from[2 + b] for a in (0, 1) for b in (0, 1)]

    loads = [
        pltpu.make_async_copy(src, dst, local_sem.at[n])
        for n, (src, dst) in enumerate(
            [
                (x_hbm.at[0], face.at[0]),
                (x_hbm.at[rows - 1], face.at[1]),
                (x_hbm.at[:, 0], face.at[2]),
                (x_hbm.at[:, cols - 1], face.at[3]),
                (x_hbm, px.at[pl.ds(1, rows), pl.ds(1, cols)]),
                (lf_hbm, lf),
                (tn_hbm, tn),
                (live_hbm, live),
                (sc_hbm, sc),
                (c_hbm, cw),
            ]
        )
    ]

    barrier = pltpu.get_barrier_semaphore()
    for k in range(1, ny):
        pl.semaphore_signal(barrier, inc=1, device_id=(i, lax.rem(j + k, ny)), device_id_type=MESH)
    for flag, device in list(zip(has_to[:2], to[:2])) + list(zip(corner_has_to, corner_to)):

        @pl.when(flag)
        def _(device=device):
            pl.semaphore_signal(barrier, inc=1, device_id=device, device_id_type=MESH)

    partners = ny - 1 + (one(low_a) + one(high_a)) * (1 + one(low_b) + one(high_b))

    for load in loads:
        load.start()

    def zero_when(flag, ref, index):
        @pl.when(jnp.logical_not(flag))
        def _():
            ref[index] = jnp.zeros(ref.at[index].shape, ref.dtype)

    inner_a, inner_b = slice(1, rows + 1), slice(1, cols + 1)
    halo_at = [
        (rows + 1, inner_b),
        (0, inner_b),
        (inner_a, cols + 1),
        (inner_a, 0),
    ]
    for d in range(4):
        zero_when(has_from[d], px, halo_at[d])
    x0[...] = jnp.zeros_like(x0)
    field[...] = jnp.zeros_like(field)

    for d in range(4):
        loads[d].wait()
    face_stage[...] = face[...].astype(F32)[:, :, 0:8, :].reshape(face_stage.shape)
    for d in range(4):
        edge[d] = face_stage[pl.ds(8 * rows * d, rows, stride=8), :].astype(BF)

    def remote(src, dst, send, recv, device):
        return pltpu.make_async_remote_copy(
            src_ref=src, dst_ref=dst, send_sem=send, recv_sem=recv, device_id=device, device_id_type=MESH
        )

    layer_copies = [
        remote(edge.at[d], halo0.at[d], h0_send.at[d], h0_recv.at[d], to[d]) for d in range(4)
    ]
    x_edges = [x_hbm.at[0], x_hbm.at[rows - 1], x_hbm.at[:, 0], x_hbm.at[:, cols - 1]]
    x_halos = [
        px.at[rows + 1, pl.ds(1, cols)],
        px.at[0, pl.ds(1, cols)],
        px.at[pl.ds(1, rows), cols + 1],
        px.at[pl.ds(1, rows), 0],
    ]
    x_copies = [
        remote(x_edges[d], x_halos[d], hx_send.at[d], hx_recv.at[d], to[d]) for d in range(4)
    ]
    two = 2 * tile_b
    lf_srcs = [lf_edge.at[0], lf_edge.at[1], lf_edge.at[2, pl.ds(0, 2 * tile_a)], lf_edge.at[3, pl.ds(0, 2 * tile_a)]]
    lf_dsts = [lf_halo.at[0], lf_halo.at[1], lf_halo.at[2, pl.ds(0, 2 * tile_a)], lf_halo.at[3, pl.ds(0, 2 * tile_a)]]
    lf_copies = [
        remote(lf_srcs[d], lf_dsts[d], lf_send.at[d], lf_recv.at[d], to[d]) for d in range(4)
    ]
    corner_rows = [0, tile_b - 8, tile_nodes - tile_b, tile_nodes - 8]
    corner_copies = [
        remote(lf.at[pl.ds(corner_rows[d], 8)], lf_corner.at[d], lc_send.at[d], lc_recv.at[d], corner_to[d])
        for d in range(4)
    ]

    def start_when(flag, copy):
        @pl.when(flag)
        def _():
            copy.start()

    pl.semaphore_wait(barrier, partners)
    for d in range(4):
        start_when(has_to[d], layer_copies[d])
    for d in range(4):
        start_when(has_to[d], x_copies[d])

    loads[5].wait()
    loads[6].wait()
    loads[7].wait()
    slot_id = lax.broadcasted_iota(jnp.int32, (1, slots), 1)
    nodes_out[...] = jnp.full(nodes_out.shape, -1, jnp.int32)
    for o in range(ny):
        count = live[0:1, o : o + 1]
        nodes_out[o, 0:1, 0:slots] = jnp.where(slot_id < count, tn[o : o + 1, :], -1)

    def row_copies(src, dst, send, recv, per_owner):
        sends, receives = [], []
        for k in range(1, ny):
            target, source = lax.rem(j + k, ny), lax.rem(j + ny - k, ny)
            sends.append(
                remote(src(target), dst(j), send.at[k - 1], recv.at[k - 1], (i, target))
            )
            receives.append(
                remote(src(target), dst(source), send.at[k - 1], recv.at[k - 1], (i, target))
            )
        return sends, receives

    node_sends, node_receives = row_copies(
        lambda o: nodes_out.at[o], lambda o: nodes_in.at[o], nd_send, nd_recv, 1
    )
    nodes_in[j] = nodes_out[j]

    lf_edge[0] = lf[0:two].astype(BF)
    lf_edge[1] = lf[tile_nodes - two : tile_nodes].astype(BF)
    for d, first in ((2, 0), (3, tile_b - 2)):
        for c in range(2):
            lf_stage[c * tile_a : (c + 1) * tile_a] = lf[pl.ds(first + c, tile_a, stride=tile_b), :]
        lf_edge[d, 0 : 2 * tile_a] = lf_stage[...].astype(BF)

    for copy in node_sends:
        copy.start()
    for d in range(4):
        start_when(has_to[d], lf_copies[d])
    for d in range(4):
        start_when(corner_has_to[d], corner_copies[d])

    loads[4].wait()
    stage[...] = px[inner_a, inner_b].astype(F32)[:, :, 0:8, :].reshape(faces * 8, width)
    x0[inner_a, 8 : 8 + cols] = stage[pl.ds(0, faces, stride=8), :].reshape(rows, cols, width)

    loads[8].wait()
    column = jnp.broadcast_to(sc[0:1, :].astype(F32), (128, faces)).T
    for part in range(faces // 128):
        face_id = lax.broadcasted_iota(jnp.int32, (faces, 128), 1) + 128 * part
        pick[:, 128 * part : 128 * (part + 1)] = (column == face_id.astype(F32)).astype(BF)

    loads[9].wait()

    half = (rows - 2) // 2
    interior(px, cw, out_ref, 1, half)

    def basal_halo(d):
        layer_copies[d].wait_recv()
        block = halo0[d].astype(F32)
        if d < 2:
            x0[(rows + 1, 0)[d], 8 : 8 + cols] = block
        else:
            at = (8 + cols, 7)[d - 2]
            x0[inner_a, at : at + 1] = block.reshape(rows, 1, width)

    for d in range(4):
        pl.when(has_from[d])(functools.partial(basal_halo, d))
    basal_terms = [
        x0[inner_a, 8 : 8 + cols].reshape(faces, width),
        stage[pl.ds(1, faces, stride=8), :],
        x0[0:rows, 8 : 8 + cols].reshape(faces, width),
        x0[2 : rows + 2, 8 : 8 + cols].reshape(faces, width),
        x0[inner_a, 7 : 7 + cols].reshape(faces, width),
        x0[inner_a, 9 : 9 + cols].reshape(faces, width),
    ]
    basal_lhs = jnp.concatenate([t.astype(BF) for t in basal_terms], axis=1)
    basal_w = jnp.concatenate([cw[0], cw[2:7].reshape(5 * width, width)], axis=0)
    basal = jnp.dot(basal_lhs, basal_w, preferred_element_type=F32).astype(BF)
    picked[...] = jnp.dot(pick[...], basal, preferred_element_type=F32).astype(BF)

    def slot_rows(ref):
        return lambda o: ref.at[pl.ds(pl.multiple_of(o * slots, slots), slots)]

    block_sends, block_receives = row_copies(
        slot_rows(picked), slot_rows(received), pk_send, pk_recv, slots
    )
    for copy in block_sends:
        copy.start()
    mine = pl.ds(pl.multiple_of(j * slots, slots), slots)
    received[mine, :] = picked[mine, :]

    interior(px, cw, out_ref, 1 + half, rows - 2 - half)

    field[2 : 2 + tile_a, 8 : 8 + tile_b] = lf[...].reshape(tile_a, tile_b, width)

    def field_halo(d):
        lf_copies[d].wait_recv()
        if d < 2:
            at = (2 + tile_a, 0)[d]
            field[at : at + 2, 8 : 8 + tile_b] = lf_halo[d].astype(F32).reshape(2, tile_b, width)
        else:
            at = (8 + tile_b, 6)[d - 2]
            block = lf_halo[d, 0 : 2 * tile_a].astype(F32)
            for c in range(2):
                field[2 : 2 + tile_a, at + c : at + c + 1] = block[
                    c * tile_a : (c + 1) * tile_a
                ].reshape(tile_a, 1, width)

    def field_corner(d):
        corner_copies[d].wait_recv()
        row, at = (2 + tile_a, 1)[d // 2], (8 + tile_b, 7)[d % 2]
        source = (0, 7)[d % 2]
        field[row, at : at + 1] = lf_corner[d, source : source + 1]

    for d in range(4):
        pl.when(has_from[d])(functools.partial(field_halo, d))
    for d in range(4):
        pl.when(corner_has_from[d])(functools.partial(field_corner, d))

    def stencil(ref, a0, na, b0, nb):
        beside = (
            ref[a0 + 1 : a0 + 1 + na, b0 : b0 + nb]
            + ref[a0 - 1 : a0 - 1 + na, b0 : b0 + nb]
            + ref[a0 : a0 + na, b0 + 1 : b0 + 1 + nb]
            + ref[a0 : a0 + na, b0 - 1 : b0 - 1 + nb]
        )
        return 1.3 * ref[a0 : a0 + na, b0 : b0 + nb] - 0.2 * beside

    first = stencil(field, 1, tile_a + 2, 7, tile_b + 2)
    row_id = lax.broadcasted_iota(jnp.int32, first.shape, 0) + i * tile_a - 1
    col_id = lax.broadcasted_iota(jnp.int32, first.shape, 1) + j * tile_b - 1
    inside = (row_id >= 0) & (row_id < nx * tile_a) & (col_id >= 0) & (col_id < ny * tile_b)
    once[:, 7 : 9 + tile_b] = jnp.where(inside, first, 0.0)
    prior[...] = stencil(once, 1, tile_a, 8, tile_b).reshape(tile_nodes, width)
    scale[...] = jnp.exp(lf[...])

    for d in range(4):
        pl.when(has_from[d])(x_copies[d].wait_recv)
    for copy in node_receives + block_receives:
        copy.wait_recv()
    def sent(d):
        layer_copies[d].wait_send()
        x_copies[d].wait_send()
        lf_copies[d].wait_send()

    for d in range(4):
        pl.when(has_to[d])(functools.partial(sent, d))
        pl.when(corner_has_to[d])(corner_copies[d].wait_send)
    for copy in node_sends + block_sends:
        copy.wait_send()


def solution(mesh):
    nx, ny = mesh.shape["gx"], mesh.shape["gy"]

    def per_device(adjoint_trace, coupling, log_friction, send_column, live_count, target_node):
        rows, cols, layers, width = adjoint_trace.shape
        tile_a, tile_b, _ = log_friction.shape
        tile_nodes = tile_a * tile_b
        faces = rows * cols
        slots = faces // ny
        vmem = pltpu.VMEM
        dma = pltpu.SemaphoreType.DMA
        hbm = pl.BlockSpec(memory_space=pltpu.HBM)
        local = pl.BlockSpec(memory_space=vmem)
        shape = jax.ShapeDtypeStruct
        held = pl.pallas_call(
            functools.partial(kernel, nx, ny),
            out_shape=(
                shape(adjoint_trace.shape, BF),
                shape((rows + 2, cols + 2, layers, width), BF),
                shape(coupling.shape, BF),
                shape((tile_nodes, width), F32),
                shape((tile_nodes, width), F32),
                shape((ny, 8, 128), jnp.int32),
                shape((faces, width), BF),
            ),
            in_specs=[hbm] * 6,
            out_specs=(local,) * 7,
            scratch_shapes=[
                vmem((tile_nodes, width), F32),
                vmem((1, faces), jnp.int32),
                vmem((1, ny), jnp.int32),
                vmem((ny, slots), jnp.int32),
                vmem((4, rows, layers, width), BF),
                vmem((4 * rows * 8, width), F32),
                vmem((faces * 8, width), F32),
                vmem((rows + 2, cols + 16, width), F32),
                vmem((4, 16, width), BF),
                vmem((4, 16, width), BF),
                vmem((2 * tile_a, width), F32),
                vmem((4, 2 * tile_b, width), BF),
                vmem((4, 2 * tile_b, width), BF),
                vmem((4, 8, width), F32),
                vmem((tile_a + 4, tile_b + 16, width), F32),
                vmem((tile_a + 2, tile_b + 16, width), F32),
                vmem((ny, 8, 128), jnp.int32),
                vmem((faces, faces), BF),
                vmem((faces, width), BF),
                dma((10,)),
                *[dma((4,)) for _ in range(8)],
                *[dma((ny - 1,)) for _ in range(4)],
            ],
            compiler_params=pltpu.CompilerParams(
                collective_id=0, has_side_effects=True, vmem_limit_bytes=24 * 2**20
            ),
            cost_estimate=pl.CostEstimate(
                flops=2 * 7 * faces * layers * width * width,
                bytes_accessed=4 * faces * layers * width,
                transcendentals=tile_nodes * width,
            ),
        )(
            *[
                pltpu.with_memory_space_constraint(operand, pltpu.HBM)
                for operand in (
                    adjoint_trace,
                    coupling,
                    log_friction.reshape(tile_nodes, width),
                    send_column.reshape(1, faces),
                    live_count.reshape(1, ny),
                    target_node.reshape(ny, slots),
                )
            ]
        )
        trace_update, gradient = pl.pallas_call(
            functools.partial(finish, ny),
            out_shape=(shape(adjoint_trace.shape, BF), shape((tile_nodes, width), F32)),
            in_specs=[local] * 7,
            out_specs=(hbm, hbm),
            scratch_shapes=[
                vmem(adjoint_trace.shape, BF),
                vmem((tile_nodes, width), F32),
                dma((8,)),
            ],
            compiler_params=pltpu.CompilerParams(vmem_limit_bytes=24 * 2**20),
        )(*held)
        return trace_update, gradient.reshape(tile_a, tile_b, width)

    in_specs = (
        P("gx", "gy", None, None),
        P(),
        P("gx", "gy", None),
        P("gx", "gy", None),
        P("gx", "gy", None),
        P("gx", "gy", None, None),
    )
    out_specs = (P("gx", "gy", None, None), P("gx", "gy", None))
    return jax.shard_map(
        per_device, mesh=mesh, in_specs=in_specs, out_specs=out_specs, check_vma=False
    )
```

```python
import functools

import jax
import jax.numpy as jnp
from jax import lax
from jax.experimental import pallas as pl
from jax.experimental.pallas import tpu as pltpu
from jax.sharding import PartitionSpec as P

MESH = pl.DeviceIdType.MESH
BF, F32 = jnp.bfloat16, jnp.float32


def product(px, cw, out_ref, a0, na, b0, nb):
    layers, width = px.shape[2:]
    own = px[pl.ds(a0 + 1, na), b0 + 1 : b0 + 1 + nb]
    count = na * nb
    wide = own.astype(F32).reshape(count, layers, width)
    layer = lax.broadcasted_iota(jnp.int32, wide.shape, 1)
    below = jnp.where(layer == 0, 0.0, pltpu.roll(wide, 1, 1)).astype(BF)
    above = jnp.where(layer == layers - 1, 0.0, pltpu.roll(wide, layers - 1, 1)).astype(BF)
    flat = lambda v: v.reshape(count * layers, width)
    terms = [
        own,
        below,
        above,
        px[pl.ds(a0, na), b0 + 1 : b0 + 1 + nb],
        px[pl.ds(a0 + 2, na), b0 + 1 : b0 + 1 + nb],
        px[pl.ds(a0 + 1, na), b0 : b0 + nb],
        px[pl.ds(a0 + 1, na), b0 + 2 : b0 + 2 + nb],
    ]
    lhs = jnp.concatenate([flat(t) for t in terms], axis=1)
    total = jnp.dot(lhs, cw[...].reshape(7 * width, width), preferred_element_type=F32)
    out_ref[pl.ds(a0, na), b0 : b0 + nb] = total.astype(BF).reshape(na, nb, layers, width)


def interior(px, cw, out_ref, first, count):
    product(px, cw, out_ref, first, count, 1, px.shape[1] - 4)


def finish(
    ny,
    inner, px, cw, scale, prior, nodes, received,
    out_hbm, grad_hbm,
    rest, grad, sem,
):
    rows, cols = inner.shape[:2]
    tile_nodes, width = scale.shape
    slots = received.shape[0] // ny
    writes = []

    def write(src, dst):
        copy = pltpu.make_async_copy(src, dst, sem.at[len(writes)])
        copy.start()
        writes.append(copy)

    def write_part(ref, a0, na, b0, nb):
        at = (pl.ds(a0, na), pl.ds(b0, nb))
        write(ref.at[at], out_hbm.at[at])

    write_part(inner, 1, rows - 2, 1, cols - 2)

    node_id = lax.broadcasted_iota(jnp.int32, (tile_nodes, slots), 0)
    misfit = jnp.zeros((tile_nodes, width), F32)
    for o in range(ny):
        onehot = (node_id == nodes[o, 0:1, 0:slots]).astype(F32).astype(BF)
        misfit = misfit + jnp.dot(
            onehot, received[o * slots : (o + 1) * slots], preferred_element_type=F32
        )
    grad[...] = scale[...] * misfit + prior[...]
    write(grad, grad_hbm)

    for part in (
        (0, 1, 0, cols),
        (rows - 1, 1, 0, cols),
        (1, rows - 2, 0, 1),
        (1, rows - 2, cols - 1, 1),
    ):
        product(px, cw, rest, *part)
        write_part(rest, *part)
    for copy in writes:
        copy.wait()


def kernel(
    nx, ny,
    x_hbm, c_hbm, lf_hbm, sc_hbm, live_hbm, tn_hbm,
    out_ref, px, cw, scale, prior, nodes_in, received,
    lf, sc, live, tn,
    side, face, face_stage, stage, x0, edge, halo0,
    lf_stage, lf_edge, lf_halo, lf_corner, field, once,
    nodes_out, pick, picked,
    local_sem, h0_send, h0_recv, hx_send, hx_recv, lf_send, lf_recv, lc_send, lc_recv,
    nd_send, nd_recv, pk_send, pk_recv,
):
    i, j = lax.axis_index("gx"), lax.axis_index("gy")
    rows, cols, layers, width = x_hbm.shape
    faces = rows * cols
    slots = faces // ny
    tile_a, tile_b = once.shape[0] - 2, cols
    tile_nodes = tile_a * tile_b
    low_a, high_a, low_b, high_b = i > 0, i < nx - 1, j > 0, j < ny - 1
    one = lambda flag: flag.astype(jnp.int32)
    up = lambda v, n: lax.rem(v + 1, n)
    down = lambda v, n: lax.rem(v + n - 1, n)
    to = [(down(i, nx), j), (up(i, nx), j), (i, down(j, ny)), (i, up(j, ny))]
    has_to = [low_a, high_a, low_b, high_b]
    has_from = [high_a, low_a, high_b, low_b]
    corner_to = [(to[a][0], to[2 + b][1]) for a in (0, 1) for b in (0, 1)]
    corner_has_to = [has_to[a] & has_to[2 + b] for a in (0, 1) for b in (0, 1)]
    corner_has_from = [has_from[a] & has_from[2 + b] for a in (0, 1) for b in (0, 1)]

    loads = [
        pltpu.make_async_copy(src, dst, local_sem.at[n])
        for n, (src, dst) in enumerate(
            [
                (x_hbm.at[0], face.at[0]),
                (x_hbm.at[rows - 1], face.at[1]),
                (x_hbm.at[:, 0], face.at[2]),
                (x_hbm.at[:, cols - 1], face.at[3]),
                (x_hbm, px.at[pl.ds(1, rows), pl.ds(1, cols)]),
                (lf_hbm, lf),
                (tn_hbm, tn),
                (live_hbm, live),
                (sc_hbm, sc),
                (c_hbm, cw),
            ]
        )
    ]

    barrier = pltpu.get_barrier_semaphore()
    for k in range(1, ny):
        pl.semaphore_signal(barrier, inc=1, device_id=(i, lax.rem(j + k, ny)), device_id_type=MESH)
    for flag, device in list(zip(has_to[:2], to[:2])) + list(zip(corner_has_to, corner_to)):

        @pl.when(flag)
        def _(device=device):
            pl.semaphore_signal(barrier, inc=1, device_id=device, device_id_type=MESH)

    partners = ny - 1 + (one(low_a) + one(high_a)) * (1 + one(low_b) + one(high_b))

    for load in loads:
        load.start()

    def zero_when(flag, ref, index):
        @pl.when(jnp.logical_not(flag))
        def _():
            ref[index] = jnp.zeros(ref.at[index].shape, ref.dtype)

    inner_a, inner_b = slice(1, rows + 1), slice(1, cols + 1)
    halo_at = [
        (rows + 1, inner_b),
        (0, inner_b),
        (inner_a, cols + 1),
        (inner_a, 0),
    ]
    for d in range(4):
        zero_when(has_from[d], px, halo_at[d])
    x0[...] = jnp.zeros_like(x0)
    field[...] = jnp.zeros_like(field)

    for d in range(4):
        loads[d].wait()
    face_stage[...] = face[...].astype(F32)[:, :, 0:8, :].reshape(face_stage.shape)
    for d in range(4):
        edge[d] = face_stage[pl.ds(8 * rows * d, rows, stride=8), :].astype(BF)

    def remote(src, dst, send, recv, device):
        return pltpu.make_async_remote_copy(
            src_ref=src, dst_ref=dst, send_sem=send, recv_sem=recv, device_id=device, device_id_type=MESH
        )

    layer_copies = [
        remote(edge.at[d], halo0.at[d], h0_send.at[d], h0_recv.at[d], to[d]) for d in range(4)
    ]
    x_halos = [
        px.at[rows + 1, pl.ds(1, cols)],
        px.at[0, pl.ds(1, cols)],
        side.at[0],
        side.at[1],
    ]
    x_copies = [
        remote(face.at[d], x_halos[d], hx_send.at[d], hx_recv.at[d], to[d]) for d in range(4)
    ]
    two = 2 * tile_b
    lf_srcs = [lf_edge.at[0], lf_edge.at[1], lf_edge.at[2, pl.ds(0, 2 * tile_a)], lf_edge.at[3, pl.ds(0, 2 * tile_a)]]
    lf_dsts = [lf_halo.at[0], lf_halo.at[1], lf_halo.at[2, pl.ds(0, 2 * tile_a)], lf_halo.at[3, pl.ds(0, 2 * tile_a)]]
    lf_copies = [
        remote(lf_srcs[d], lf_dsts[d], lf_send.at[d], lf_recv.at[d], to[d]) for d in range(4)
    ]
    corner_rows = [0, tile_b - 8, tile_nodes - tile_b, tile_nodes - 8]
    corner_copies = [
        remote(lf.at[pl.ds(corner_rows[d], 8)], lf_corner.at[d], lc_send.at[d], lc_recv.at[d], corner_to[d])
        for d in range(4)
    ]

    def start_when(flag, copy):
        @pl.when(flag)
        def _():
            copy.start()

    pl.semaphore_wait(barrier, partners)
    for d in range(4):
        start_when(has_to[d], layer_copies[d])
    for d in range(4):
        start_when(has_to[d], x_copies[d])

    loads[5].wait()
    loads[6].wait()
    loads[7].wait()
    slot_id = lax.broadcasted_iota(jnp.int32, (1, slots), 1)
    nodes_out[...] = jnp.full(nodes_out.shape, -1, jnp.int32)
    for o in range(ny):
        count = live[0:1, o : o + 1]
        nodes_out[o, 0:1, 0:slots] = jnp.where(slot_id < count, tn[o : o + 1, :], -1)

    def row_copies(src, dst, send, recv, per_owner):
        sends, receives = [], []
        for k in range(1, ny):
            target, source = lax.rem(j + k, ny), lax.rem(j + ny - k, ny)
            sends.append(
                remote(src(target), dst(j), send.at[k - 1], recv.at[k - 1], (i, target))
            )
            receives.append(
                remote(src(target), dst(source), send.at[k - 1], recv.at[k - 1], (i, target))
            )
        return sends, receives

    node_sends, node_receives = row_copies(
        lambda o: nodes_out.at[o], lambda o: nodes_in.at[o], nd_send, nd_recv, 1
    )
    nodes_in[j] = nodes_out[j]

    lf_edge[0] = lf[0:two].astype(BF)
    lf_edge[1] = lf[tile_nodes - two : tile_nodes].astype(BF)
    for d, first in ((2, 0), (3, tile_b - 2)):
        for c in range(2):
            lf_stage[c * tile_a : (c + 1) * tile_a] = lf[pl.ds(first + c, tile_a, stride=tile_b), :]
        lf_edge[d, 0 : 2 * tile_a] = lf_stage[...].astype(BF)

    for copy in node_sends:
        copy.start()
    for d in range(4):
        start_when(has_to[d], lf_copies[d])
    for d in range(4):
        start_when(corner_has_to[d], corner_copies[d])

    loads[4].wait()
    stage[...] = px[inner_a, inner_b].astype(F32)[:, :, 0:8, :].reshape(faces * 8, width)
    x0[inner_a, 8 : 8 + cols] = stage[pl.ds(0, faces, stride=8), :].reshape(rows, cols, width)

    loads[8].wait()
    column = jnp.broadcast_to(sc[0:1, :].astype(F32), (128, faces)).T
    for part in range(faces // 128):
        face_id = lax.broadcasted_iota(jnp.int32, (faces, 128), 1) + 128 * part
        pick[:, 128 * part : 128 * (part + 1)] = (column == face_id.astype(F32)).astype(BF)

    loads[9].wait()

    half = (rows - 2) // 2
    interior(px, cw, out_ref, 1, half)

    def basal_halo(d):
        layer_copies[d].wait_recv()
        block = halo0[d].astype(F32)
        if d < 2:
            x0[(rows + 1, 0)[d], 8 : 8 + cols] = block
        else:
            at = (8 + cols, 7)[d - 2]
            x0[inner_a, at : at + 1] = block.reshape(rows, 1, width)

    for d in range(4):
        pl.when(has_from[d])(functools.partial(basal_halo, d))
    basal_terms = [
        x0[inner_a, 8 : 8 + cols].reshape(faces, width),
        stage[pl.ds(1, faces, stride=8), :],
        x0[0:rows, 8 : 8 + cols].reshape(faces, width),
        x0[2 : rows + 2, 8 : 8 + cols].reshape(faces, width),
        x0[inner_a, 7 : 7 + cols].reshape(faces, width),
        x0[inner_a, 9 : 9 + cols].reshape(faces, width),
    ]
    basal_lhs = jnp.concatenate([t.astype(BF) for t in basal_terms], axis=1)
    basal_w = jnp.concatenate([cw[0], cw[2:7].reshape(5 * width, width)], axis=0)
    basal = jnp.dot(basal_lhs, basal_w, preferred_element_type=F32).astype(BF)
    picked[...] = jnp.dot(pick[...], basal, preferred_element_type=F32).astype(BF)

    def slot_rows(ref):
        return lambda o: ref.at[pl.ds(pl.multiple_of(o * slots, slots), slots)]

    block_sends, block_receives = row_copies(
        slot_rows(picked), slot_rows(received), pk_send, pk_recv, slots
    )
    for copy in block_sends:
        copy.start()
    mine = pl.ds(pl.multiple_of(j * slots, slots), slots)
    received[mine, :] = picked[mine, :]

    interior(px, cw, out_ref, 1 + half, rows - 2 - half)

    field[2 : 2 + tile_a, 8 : 8 + tile_b] = lf[...].reshape(tile_a, tile_b, width)

    def field_halo(d):
        lf_copies[d].wait_recv()
        if d < 2:
            at = (2 + tile_a, 0)[d]
            field[at : at + 2, 8 : 8 + tile_b] = lf_halo[d].astype(F32).reshape(2, tile_b, width)
        else:
            at = (8 + tile_b, 6)[d - 2]
            block = lf_halo[d, 0 : 2 * tile_a].astype(F32)
            for c in range(2):
                field[2 : 2 + tile_a, at + c : at + c + 1] = block[
                    c * tile_a : (c + 1) * tile_a
                ].reshape(tile_a, 1, width)

    def field_corner(d):
        corner_copies[d].wait_recv()
        row, at = (2 + tile_a, 1)[d // 2], (8 + tile_b, 7)[d % 2]
        source = (0, 7)[d % 2]
        field[row, at : at + 1] = lf_corner[d, source : source + 1]

    for d in range(4):
        pl.when(has_from[d])(functools.partial(field_halo, d))
    for d in range(4):
        pl.when(corner_has_from[d])(functools.partial(field_corner, d))

    def stencil(ref, a0, na, b0, nb):
        beside = (
            ref[a0 + 1 : a0 + 1 + na, b0 : b0 + nb]
            + ref[a0 - 1 : a0 - 1 + na, b0 : b0 + nb]
            + ref[a0 : a0 + na, b0 + 1 : b0 + 1 + nb]
            + ref[a0 : a0 + na, b0 - 1 : b0 - 1 + nb]
        )
        return 1.3 * ref[a0 : a0 + na, b0 : b0 + nb] - 0.2 * beside

    first = stencil(field, 1, tile_a + 2, 7, tile_b + 2)
    row_id = lax.broadcasted_iota(jnp.int32, first.shape, 0) + i * tile_a - 1
    col_id = lax.broadcasted_iota(jnp.int32, first.shape, 1) + j * tile_b - 1
    inside = (row_id >= 0) & (row_id < nx * tile_a) & (col_id >= 0) & (col_id < ny * tile_b)
    once[:, 7 : 9 + tile_b] = jnp.where(inside, first, 0.0)
    prior[...] = stencil(once, 1, tile_a, 8, tile_b).reshape(tile_nodes, width)
    scale[...] = jnp.exp(lf[...])

    def side_halo(d):
        x_copies[d].wait_recv()
        px[halo_at[d]] = side[d - 2]

    for d in range(2):
        pl.when(has_from[d])(x_copies[d].wait_recv)
    for d in range(2, 4):
        pl.when(has_from[d])(functools.partial(side_halo, d))
    for copy in node_receives + block_receives:
        copy.wait_recv()
    def sent(d):
        layer_copies[d].wait_send()
        x_copies[d].wait_send()
        lf_copies[d].wait_send()

    for d in range(4):
        pl.when(has_to[d])(functools.partial(sent, d))
        pl.when(corner_has_to[d])(corner_copies[d].wait_send)
    for copy in node_sends + block_sends:
        copy.wait_send()


def solution(mesh):
    nx, ny = mesh.shape["gx"], mesh.shape["gy"]

    def per_device(adjoint_trace, coupling, log_friction, send_column, live_count, target_node):
        rows, cols, layers, width = adjoint_trace.shape
        tile_a, tile_b, _ = log_friction.shape
        tile_nodes = tile_a * tile_b
        faces = rows * cols
        slots = faces // ny
        vmem = pltpu.VMEM
        dma = pltpu.SemaphoreType.DMA
        hbm = pl.BlockSpec(memory_space=pltpu.HBM)
        local = pl.BlockSpec(memory_space=vmem)
        shape = jax.ShapeDtypeStruct
        held = pl.pallas_call(
            functools.partial(kernel, nx, ny),
            out_shape=(
                shape(adjoint_trace.shape, BF),
                shape((rows + 2, cols + 2, layers, width), BF),
                shape(coupling.shape, BF),
                shape((tile_nodes, width), F32),
                shape((tile_nodes, width), F32),
                shape((ny, 8, 128), jnp.int32),
                shape((faces, width), BF),
            ),
            in_specs=[hbm] * 6,
            out_specs=(local,) * 7,
            scratch_shapes=[
                vmem((tile_nodes, width), F32),
                vmem((1, faces), jnp.int32),
                vmem((1, ny), jnp.int32),
                vmem((ny, slots), jnp.int32),
                vmem((2, rows, layers, width), BF),
                vmem((4, rows, layers, width), BF),
                vmem((4 * rows * 8, width), F32),
                vmem((faces * 8, width), F32),
                vmem((rows + 2, cols + 16, width), F32),
                vmem((4, 16, width), BF),
                vmem((4, 16, width), BF),
                vmem((2 * tile_a, width), F32),
                vmem((4, 2 * tile_b, width), BF),
                vmem((4, 2 * tile_b, width), BF),
                vmem((4, 8, width), F32),
                vmem((tile_a + 4, tile_b + 16, width), F32),
                vmem((tile_a + 2, tile_b + 16, width), F32),
                vmem((ny, 8, 128), jnp.int32),
                vmem((faces, faces), BF),
                vmem((faces, width), BF),
                dma((10,)),
                *[dma((4,)) for _ in range(8)],
                *[dma((ny - 1,)) for _ in range(4)],
            ],
            compiler_params=pltpu.CompilerParams(
                collective_id=0, has_side_effects=True, vmem_limit_bytes=24 * 2**20
            ),
            cost_estimate=pl.CostEstimate(
                flops=2 * 7 * faces * layers * width * width,
                bytes_accessed=4 * faces * layers * width,
                transcendentals=tile_nodes * width,
            ),
        )(
            *[
                pltpu.with_memory_space_constraint(operand, pltpu.HBM)
                for operand in (
                    adjoint_trace,
                    coupling,
                    log_friction.reshape(tile_nodes, width),
                    send_column.reshape(1, faces),
                    live_count.reshape(1, ny),
                    target_node.reshape(ny, slots),
                )
            ]
        )
        trace_update, gradient = pl.pallas_call(
            functools.partial(finish, ny),
            out_shape=(shape(adjoint_trace.shape, BF), shape((tile_nodes, width), F32)),
            in_specs=[local] * 7,
            out_specs=(hbm, hbm),
            scratch_shapes=[
                vmem(adjoint_trace.shape, BF),
                vmem((tile_nodes, width), F32),
                dma((8,)),
            ],
            compiler_params=pltpu.CompilerParams(vmem_limit_bytes=24 * 2**20),
        )(*held)
        return trace_update, gradient.reshape(tile_a, tile_b, width)

    in_specs = (
        P("gx", "gy", None, None),
        P(),
        P("gx", "gy", None),
        P("gx", "gy", None),
        P("gx", "gy", None),
        P("gx", "gy", None, None),
    )
    out_specs = (P("gx", "gy", None, None), P("gx", "gy", None))
    return jax.shard_map(
        per_device, mesh=mesh, in_specs=in_specs, out_specs=out_specs, check_vma=False
    )
```

```python
import functools

import jax
import jax.numpy as jnp
from jax import lax
from jax.experimental import pallas as pl
from jax.experimental.pallas import tpu as pltpu
from jax.sharding import PartitionSpec as P

MESH = pl.DeviceIdType.MESH
BF, F32 = jnp.bfloat16, jnp.float32


def product(px, cw, out_ref, a0, na, b0, nb):
    layers, width = px.shape[2:]
    own = px[pl.ds(a0 + 1, na), b0 + 1 : b0 + 1 + nb]
    count = na * nb
    wide = own.astype(F32).reshape(count, layers, width)
    layer = lax.broadcasted_iota(jnp.int32, wide.shape, 1)
    below = jnp.where(layer == 0, 0.0, pltpu.roll(wide, 1, 1)).astype(BF)
    above = jnp.where(layer == layers - 1, 0.0, pltpu.roll(wide, layers - 1, 1)).astype(BF)
    flat = lambda v: v.reshape(count * layers, width)
    terms = [
        own,
        below,
        above,
        px[pl.ds(a0, na), b0 + 1 : b0 + 1 + nb],
        px[pl.ds(a0 + 2, na), b0 + 1 : b0 + 1 + nb],
        px[pl.ds(a0 + 1, na), b0 : b0 + nb],
        px[pl.ds(a0 + 1, na), b0 + 2 : b0 + 2 + nb],
    ]
    lhs = jnp.concatenate([flat(t) for t in terms], axis=1)
    total = jnp.dot(lhs, cw[...].reshape(7 * width, width), preferred_element_type=F32)
    out_ref[pl.ds(a0, na), b0 : b0 + nb] = total.astype(BF).reshape(na, nb, layers, width)


def interior(px, cw, out_ref, first, count):
    product(px, cw, out_ref, first, count, 1, px.shape[1] - 4)


def finish(
    ny,
    inner, px, cw, scale, prior, nodes, received,
    out_hbm, grad_hbm,
    rest, grad, sem,
):
    rows, cols = inner.shape[:2]
    tile_nodes, width = scale.shape
    slots = received.shape[0] // ny
    writes = []

    def write(src, dst):
        copy = pltpu.make_async_copy(src, dst, sem.at[len(writes)])
        copy.start()
        writes.append(copy)

    def write_part(ref, a0, na, b0, nb):
        at = (pl.ds(a0, na), pl.ds(b0, nb))
        write(ref.at[at], out_hbm.at[at])

    write_part(inner, 1, rows - 2, 1, cols - 2)

    node_id = lax.broadcasted_iota(jnp.int32, (tile_nodes, slots), 0)
    misfit = jnp.zeros((tile_nodes, width), F32)
    for o in range(ny):
        onehot = (node_id == nodes[o, 0:1, 0:slots]).astype(F32).astype(BF)
        misfit = misfit + jnp.dot(
            onehot, received[o * slots : (o + 1) * slots], preferred_element_type=F32
        )
    grad[...] = scale[...] * misfit + prior[...]
    write(grad, grad_hbm)

    for part in (
        (0, 1, 0, cols),
        (rows - 1, 1, 0, cols),
        (1, rows - 2, 0, 1),
        (1, rows - 2, cols - 1, 1),
    ):
        product(px, cw, rest, *part)
        write_part(rest, *part)
    for copy in writes:
        copy.wait()


def kernel(
    nx, ny,
    x_hbm, c_hbm, lf_hbm, sc_hbm, live_hbm, tn_hbm,
    out_ref, px, cw, scale, prior, nodes_in, received,
    lf, sc, live, tn,
    side, face, face_stage, stage, x0, edge, halo0,
    lf_stage, lf_edge, lf_halo, lf_corner, field, once,
    nodes_out, pick, picked,
    local_sem, h0_send, h0_recv, hx_send, hx_recv, lf_send, lf_recv, lc_send, lc_recv,
    nd_send, nd_recv, pk_send, pk_recv,
):
    i, j = lax.axis_index("gx"), lax.axis_index("gy")
    rows, cols, layers, width = x_hbm.shape
    faces = rows * cols
    slots = faces // ny
    tile_a, tile_b = once.shape[0] - 2, cols
    tile_nodes = tile_a * tile_b
    low_a, high_a, low_b, high_b = i > 0, i < nx - 1, j > 0, j < ny - 1
    one = lambda flag: flag.astype(jnp.int32)
    up = lambda v, n: lax.rem(v + 1, n)
    down = lambda v, n: lax.rem(v + n - 1, n)
    to = [(down(i, nx), j), (up(i, nx), j), (i, down(j, ny)), (i, up(j, ny))]
    has_to = [low_a, high_a, low_b, high_b]
    has_from = [high_a, low_a, high_b, low_b]
    corner_to = [(to[a][0], to[2 + b][1]) for a in (0, 1) for b in (0, 1)]
    corner_has_to = [has_to[a] & has_to[2 + b] for a in (0, 1) for b in (0, 1)]
    corner_has_from = [has_from[a] & has_from[2 + b] for a in (0, 1) for b in (0, 1)]

    loads = [
        pltpu.make_async_copy(src, dst, local_sem.at[n])
        for n, (src, dst) in enumerate(
            [
                (x_hbm.at[0], face.at[0]),
                (x_hbm.at[rows - 1], face.at[1]),
                (x_hbm.at[:, 0], face.at[2]),
                (x_hbm.at[:, cols - 1], face.at[3]),
                (x_hbm, px.at[pl.ds(1, rows), pl.ds(1, cols)]),
                (lf_hbm, lf),
                (tn_hbm, tn),
                (live_hbm, live),
                (sc_hbm, sc),
                (c_hbm, cw),
            ]
        )
    ]

    barrier = pltpu.get_barrier_semaphore()
    for k in range(1, ny):
        pl.semaphore_signal(barrier, inc=1, device_id=(i, lax.rem(j + k, ny)), device_id_type=MESH)
    for flag, device in list(zip(has_to[:2], to[:2])) + list(zip(corner_has_to, corner_to)):

        @pl.when(flag)
        def _(device=device):
            pl.semaphore_signal(barrier, inc=1, device_id=device, device_id_type=MESH)

    partners = ny - 1 + (one(low_a) + one(high_a)) * (1 + one(low_b) + one(high_b))

    for n in (0, 1, 2, 3, 5, 4, 6, 7, 8, 9):
        loads[n].start()

    def zero_when(flag, ref, index):
        @pl.when(jnp.logical_not(flag))
        def _():
            ref[index] = jnp.zeros(ref.at[index].shape, ref.dtype)

    inner_a, inner_b = slice(1, rows + 1), slice(1, cols + 1)
    halo_at = [
        (rows + 1, inner_b),
        (0, inner_b),
        (inner_a, cols + 1),
        (inner_a, 0),
    ]
    for d in range(4):
        zero_when(has_from[d], px, halo_at[d])
    x0[...] = jnp.zeros_like(x0)
    field[...] = jnp.zeros_like(field)

    for d in range(4):
        loads[d].wait()
    face_stage[...] = face[...].astype(F32)[:, :, 0:8, :].reshape(face_stage.shape)
    for d in range(4):
        edge[d] = face_stage[pl.ds(8 * rows * d, rows, stride=8), :].astype(BF)

    def remote(src, dst, send, recv, device):
        return pltpu.make_async_remote_copy(
            src_ref=src, dst_ref=dst, send_sem=send, recv_sem=recv, device_id=device, device_id_type=MESH
        )

    layer_copies = [
        remote(edge.at[d], halo0.at[d], h0_send.at[d], h0_recv.at[d], to[d]) for d in range(4)
    ]
    x_halos = [
        px.at[rows + 1, pl.ds(1, cols)],
        px.at[0, pl.ds(1, cols)],
        side.at[0],
        side.at[1],
    ]
    x_copies = [
        remote(face.at[d], x_halos[d], hx_send.at[d], hx_recv.at[d], to[d]) for d in range(4)
    ]
    two = 2 * tile_b
    lf_srcs = [lf_edge.at[0], lf_edge.at[1], lf_edge.at[2, pl.ds(0, 2 * tile_a)], lf_edge.at[3, pl.ds(0, 2 * tile_a)]]
    lf_dsts = [lf_halo.at[0], lf_halo.at[1], lf_halo.at[2, pl.ds(0, 2 * tile_a)], lf_halo.at[3, pl.ds(0, 2 * tile_a)]]
    lf_copies = [
        remote(lf_srcs[d], lf_dsts[d], lf_send.at[d], lf_recv.at[d], to[d]) for d in range(4)
    ]
    corner_rows = [0, tile_b - 8, tile_nodes - tile_b, tile_nodes - 8]
    corner_copies = [
        remote(lf.at[pl.ds(corner_rows[d], 8)], lf_corner.at[d], lc_send.at[d], lc_recv.at[d], corner_to[d])
        for d in range(4)
    ]

    def start_when(flag, copy):
        @pl.when(flag)
        def _():
            copy.start()

    loads[5].wait()
    lf_edge[0] = lf[0:two].astype(BF)
    lf_edge[1] = lf[tile_nodes - two : tile_nodes].astype(BF)
    for d, first in ((2, 0), (3, tile_b - 2)):
        for c in range(2):
            lf_stage[c * tile_a : (c + 1) * tile_a] = lf[pl.ds(first + c, tile_a, stride=tile_b), :]
        lf_edge[d, 0 : 2 * tile_a] = lf_stage[...].astype(BF)

    pl.semaphore_wait(barrier, partners)
    for d in range(4):
        start_when(has_to[d], layer_copies[d])
    for d in range(4):
        start_when(has_to[d], lf_copies[d])
    for d in range(4):
        start_when(corner_has_to[d], corner_copies[d])
    for d in range(4):
        start_when(has_to[d], x_copies[d])

    loads[6].wait()
    loads[7].wait()
    slot_id = lax.broadcasted_iota(jnp.int32, (1, slots), 1)
    nodes_out[...] = jnp.full(nodes_out.shape, -1, jnp.int32)
    for o in range(ny):
        count = live[0:1, o : o + 1]
        nodes_out[o, 0:1, 0:slots] = jnp.where(slot_id < count, tn[o : o + 1, :], -1)

    def row_copies(src, dst, send, recv, per_owner):
        sends, receives = [], []
        for k in range(1, ny):
            target, source = lax.rem(j + k, ny), lax.rem(j + ny - k, ny)
            sends.append(
                remote(src(target), dst(j), send.at[k - 1], recv.at[k - 1], (i, target))
            )
            receives.append(
                remote(src(target), dst(source), send.at[k - 1], recv.at[k - 1], (i, target))
            )
        return sends, receives

    node_sends, node_receives = row_copies(
        lambda o: nodes_out.at[o], lambda o: nodes_in.at[o], nd_send, nd_recv, 1
    )
    nodes_in[j] = nodes_out[j]

    for copy in node_sends:
        copy.start()

    loads[4].wait()
    stage[...] = px[inner_a, inner_b].astype(F32)[:, :, 0:8, :].reshape(faces * 8, width)
    x0[inner_a, 8 : 8 + cols] = stage[pl.ds(0, faces, stride=8), :].reshape(rows, cols, width)

    loads[8].wait()
    column = jnp.broadcast_to(sc[0:1, :].astype(F32), (128, faces)).T
    for part in range(faces // 128):
        face_id = lax.broadcasted_iota(jnp.int32, (faces, 128), 1) + 128 * part
        pick[:, 128 * part : 128 * (part + 1)] = (column == face_id.astype(F32)).astype(BF)

    loads[9].wait()

    half = (rows - 2) // 2
    interior(px, cw, out_ref, 1, half)

    def basal_halo(d):
        layer_copies[d].wait_recv()
        block = halo0[d].astype(F32)
        if d < 2:
            x0[(rows + 1, 0)[d], 8 : 8 + cols] = block
        else:
            at = (8 + cols, 7)[d - 2]
            x0[inner_a, at : at + 1] = block.reshape(rows, 1, width)

    for d in range(4):
        pl.when(has_from[d])(functools.partial(basal_halo, d))
    basal_terms = [
        x0[inner_a, 8 : 8 + cols].reshape(faces, width),
        stage[pl.ds(1, faces, stride=8), :],
        x0[0:rows, 8 : 8 + cols].reshape(faces, width),
        x0[2 : rows + 2, 8 : 8 + cols].reshape(faces, width),
        x0[inner_a, 7 : 7 + cols].reshape(faces, width),
        x0[inner_a, 9 : 9 + cols].reshape(faces, width),
    ]
    basal_lhs = jnp.concatenate([t.astype(BF) for t in basal_terms], axis=1)
    basal_w = jnp.concatenate([cw[0], cw[2:7].reshape(5 * width, width)], axis=0)
    basal = jnp.dot(basal_lhs, basal_w, preferred_element_type=F32).astype(BF)
    picked[...] = jnp.dot(pick[...], basal, preferred_element_type=F32).astype(BF)

    def slot_rows(ref):
        return lambda o: ref.at[pl.ds(pl.multiple_of(o * slots, slots), slots)]

    block_sends, block_receives = row_copies(
        slot_rows(picked), slot_rows(received), pk_send, pk_recv, slots
    )
    for copy in block_sends:
        copy.start()
    mine = pl.ds(pl.multiple_of(j * slots, slots), slots)
    received[mine, :] = picked[mine, :]

    interior(px, cw, out_ref, 1 + half, rows - 2 - half)

    field[2 : 2 + tile_a, 8 : 8 + tile_b] = lf[...].reshape(tile_a, tile_b, width)

    def field_halo(d):
        lf_copies[d].wait_recv()
        if d < 2:
            at = (2 + tile_a, 0)[d]
            field[at : at + 2, 8 : 8 + tile_b] = lf_halo[d].astype(F32).reshape(2, tile_b, width)
        else:
            at = (8 + tile_b, 6)[d - 2]
            block = lf_halo[d, 0 : 2 * tile_a].astype(F32)
            for c in range(2):
                field[2 : 2 + tile_a, at + c : at + c + 1] = block[
                    c * tile_a : (c + 1) * tile_a
                ].reshape(tile_a, 1, width)

    def field_corner(d):
        corner_copies[d].wait_recv()
        row, at = (2 + tile_a, 1)[d // 2], (8 + tile_b, 7)[d % 2]
        source = (0, 7)[d % 2]
        field[row, at : at + 1] = lf_corner[d, source : source + 1]

    for d in range(4):
        pl.when(has_from[d])(functools.partial(field_halo, d))
    for d in range(4):
        pl.when(corner_has_from[d])(functools.partial(field_corner, d))

    def stencil(ref, a0, na, b0, nb):
        beside = (
            ref[a0 + 1 : a0 + 1 + na, b0 : b0 + nb]
            + ref[a0 - 1 : a0 - 1 + na, b0 : b0 + nb]
            + ref[a0 : a0 + na, b0 + 1 : b0 + 1 + nb]
            + ref[a0 : a0 + na, b0 - 1 : b0 - 1 + nb]
        )
        return 1.3 * ref[a0 : a0 + na, b0 : b0 + nb] - 0.2 * beside

    first = stencil(field, 1, tile_a + 2, 7, tile_b + 2)
    row_id = lax.broadcasted_iota(jnp.int32, first.shape, 0) + i * tile_a - 1
    col_id = lax.broadcasted_iota(jnp.int32, first.shape, 1) + j * tile_b - 1
    inside = (row_id >= 0) & (row_id < nx * tile_a) & (col_id >= 0) & (col_id < ny * tile_b)
    once[:, 7 : 9 + tile_b] = jnp.where(inside, first, 0.0)
    prior[...] = stencil(once, 1, tile_a, 8, tile_b).reshape(tile_nodes, width)
    scale[...] = jnp.exp(lf[...])

    def side_halo(d):
        x_copies[d].wait_recv()
        px[halo_at[d]] = side[d - 2]

    for d in range(2):
        pl.when(has_from[d])(x_copies[d].wait_recv)
    for d in range(2, 4):
        pl.when(has_from[d])(functools.partial(side_halo, d))
    for copy in node_receives + block_receives:
        copy.wait_recv()
    def sent(d):
        layer_copies[d].wait_send()
        x_copies[d].wait_send()
        lf_copies[d].wait_send()

    for d in range(4):
        pl.when(has_to[d])(functools.partial(sent, d))
        pl.when(corner_has_to[d])(corner_copies[d].wait_send)
    for copy in node_sends + block_sends:
        copy.wait_send()


def solution(mesh):
    nx, ny = mesh.shape["gx"], mesh.shape["gy"]

    def per_device(adjoint_trace, coupling, log_friction, send_column, live_count, target_node):
        rows, cols, layers, width = adjoint_trace.shape
        tile_a, tile_b, _ = log_friction.shape
        tile_nodes = tile_a * tile_b
        faces = rows * cols
        slots = faces // ny
        vmem = pltpu.VMEM
        dma = pltpu.SemaphoreType.DMA
        hbm = pl.BlockSpec(memory_space=pltpu.HBM)
        local = pl.BlockSpec(memory_space=vmem)
        shape = jax.ShapeDtypeStruct
        held = pl.pallas_call(
            functools.partial(kernel, nx, ny),
            out_shape=(
                shape(adjoint_trace.shape, BF),
                shape((rows + 2, cols + 2, layers, width), BF),
                shape(coupling.shape, BF),
                shape((tile_nodes, width), F32),
                shape((tile_nodes, width), F32),
                shape((ny, 8, 128), jnp.int32),
                shape((faces, width), BF),
            ),
            in_specs=[hbm] * 6,
            out_specs=(local,) * 7,
            scratch_shapes=[
                vmem((tile_nodes, width), F32),
                vmem((1, faces), jnp.int32),
                vmem((1, ny), jnp.int32),
                vmem((ny, slots), jnp.int32),
                vmem((2, rows, layers, width), BF),
                vmem((4, rows, layers, width), BF),
                vmem((4 * rows * 8, width), F32),
                vmem((faces * 8, width), F32),
                vmem((rows + 2, cols + 16, width), F32),
                vmem((4, 16, width), BF),
                vmem((4, 16, width), BF),
                vmem((2 * tile_a, width), F32),
                vmem((4, 2 * tile_b, width), BF),
                vmem((4, 2 * tile_b, width), BF),
                vmem((4, 8, width), F32),
                vmem((tile_a + 4, tile_b + 16, width), F32),
                vmem((tile_a + 2, tile_b + 16, width), F32),
                vmem((ny, 8, 128), jnp.int32),
                vmem((faces, faces), BF),
                vmem((faces, width), BF),
                dma((10,)),
                *[dma((4,)) for _ in range(8)],
                *[dma((ny - 1,)) for _ in range(4)],
            ],
            compiler_params=pltpu.CompilerParams(
                collective_id=0, has_side_effects=True, vmem_limit_bytes=24 * 2**20
            ),
            cost_estimate=pl.CostEstimate(
                flops=2 * 7 * faces * layers * width * width,
                bytes_accessed=4 * faces * layers * width,
                transcendentals=tile_nodes * width,
            ),
        )(
            *[
                pltpu.with_memory_space_constraint(operand, pltpu.HBM)
                for operand in (
                    adjoint_trace,
                    coupling,
                    log_friction.reshape(tile_nodes, width),
                    send_column.reshape(1, faces),
                    live_count.reshape(1, ny),
                    target_node.reshape(ny, slots),
                )
            ]
        )
        trace_update, gradient = pl.pallas_call(
            functools.partial(finish, ny),
            out_shape=(shape(adjoint_trace.shape, BF), shape((tile_nodes, width), F32)),
            in_specs=[local] * 7,
            out_specs=(hbm, hbm),
            scratch_shapes=[
                vmem(adjoint_trace.shape, BF),
                vmem((tile_nodes, width), F32),
                dma((8,)),
            ],
            compiler_params=pltpu.CompilerParams(vmem_limit_bytes=24 * 2**20),
        )(*held)
        return trace_update, gradient.reshape(tile_a, tile_b, width)

    in_specs = (
        P("gx", "gy", None, None),
        P(),
        P("gx", "gy", None),
        P("gx", "gy", None),
        P("gx", "gy", None),
        P("gx", "gy", None, None),
    )
    out_specs = (P("gx", "gy", None, None), P("gx", "gy", None))
    return jax.shard_map(
        per_device, mesh=mesh, in_specs=in_specs, out_specs=out_specs, check_vma=False
    )
```
